128 devices in a mesh: row: 4 (over z), col: 32 (over x, y, core).
Axes of the slice: x: 4, y: 4, z: 4, core: 2. Of those that a mesh axis runs over, the one named last changes fastest.
Arguments:
- evecs: float32 [1024, 65536], P('col', 'row'), may hold values from -6 to 6
- v_first: float32 [256, 65536], P('col', 'row'), may hold values from -0.046875 to 0.046875
- v_second: float32 [256, 65536], P('col', 'row'), may hold values from -0.046875 to 0.046875
- t_first: float32 [256, 256], replicated, may hold values from -0.5 to 2, as said below
- t_second: float32 [256, 256], replicated, may hold values from -0.5 to 2, as said below
Outputs:
- basis: float32 [1024, 65536], P('col', 'row')
The draws below stay inside these ranges and needn't reach their ends.
Inputs may be any that keep to these rules, and one draw needn't show every extreme that they name: `t_first`: upper triangular, with diagonal entries between 0.5 and 2. `t_second`: upper triangular, with diagonal entries between 0.5 and 2.
All inputs are finite; a program needn't handle non-finite values.
Results may differ from the reference program's by a relative error of at most 0.00016.
Values sent between devices are 32-bit elements; how exact they have to be, the bound alone decides.
A program may use at most 128 MiB of HBM per device.

```python
import jax
import jax.numpy as jnp
from jax import lax

K = 1024
NB = 256
ROWS = 65536


def triangle(key):
    key_diag, key_off = jax.random.split(key)
    diag_vals = jnp.exp(jax.random.uniform(key_diag, (NB,), jnp.float32, jnp.log(0.5), jnp.log(2.0)))
    off_vals = jnp.clip(0.1 * jax.random.normal(key_off, (NB, NB), jnp.float32), -0.5, 0.5)
    return jnp.triu(off_vals, 1) + jnp.diag(diag_vals)


def draw_t_first(key, part):
    key = jax.random.fold_in(key, 11)
    return triangle(key)


def draw_t_second(key, part):
    key = jax.random.fold_in(key, 23)
    return triangle(key)


def level_of(stream_key, extent, cuts, smallest, top_value):
    factor_of, own = 1.0, jax.random.fold_in(stream_key, 6)
    for axis_at, parts in cuts:
        heights = jnp.exp(jax.random.uniform(jax.random.fold_in(own, axis_at), (parts,), jnp.float32, smallest / len(cuts), top_value / len(cuts)))
        factor_of = factor_of * jnp.repeat(heights, extent[axis_at] // parts).reshape([-1 if axis == axis_at else 1 for axis in range(len(extent))])
    return factor_of


def normal_values(key, extent, spread, limit, pieces=(), held_as=jnp.bfloat16):
    gain = level_of(key, extent, pieces, -0.22, 0.18) if pieces else 1.0
    entries = jax.random.normal(key, extent, jnp.float32) * spread * gain
    return jnp.minimum(jnp.maximum(entries, -limit), limit).astype(held_as)


def setup_inputs(seed: int = 0) -> dict:
    splits = jax.random.split(jax.random.key(seed), 6)
    evecs = normal_values(splits[0], (K, ROWS), 1.0, 6.0, ((0, 32), (1, 4)), jnp.float32)
    v_first = normal_values(splits[1], (NB, ROWS), (ROWS // 4) ** -0.5, 0.046875, ((0, 32), (1, 4)), jnp.float32)
    v_second = normal_values(splits[2], (NB, ROWS), (ROWS // 4) ** -0.5, 0.046875, ((0, 32), (1, 4)), jnp.float32)
    t_first = draw_t_first(jax.random.fold_in(splits[5], 71), 0)
    t_second = draw_t_second(jax.random.fold_in(splits[5], 71), 0)
    return dict(evecs=evecs, v_first=v_first, v_second=v_second, t_first=t_first, t_second=t_second)


def dot_high(left, right):
    return jnp.dot(left, right, precision=lax.Precision.HIGHEST, preferred_element_type=jnp.float32)


def apply_panel(matrix, vectors, factor):
    products = dot_high(vectors, matrix.T)
    return matrix - dot_high(dot_high(factor, products).T, vectors)


def reference(evecs, v_first, v_second, t_first, t_second):
    middle = apply_panel(evecs, v_second, t_second)
    return apply_panel(middle, v_first, t_first)
```

```python
import jax
import jax.numpy as jnp
from jax import lax
from jax.experimental import pallas as pl
from jax.experimental.pallas import tpu as pltpu
from jax.sharding import PartitionSpec as P

MESH = pl.DeviceIdType.MESH
F32 = jnp.float32
BF16 = jnp.bfloat16
HIGHEST = lax.Precision.HIGHEST

SIDE = 4
HALF = 8192
PART = HALF // SIDE
MINE = 32
TILE = 1024
OFFSETS = (1, 3, 2)


def inner(left, right):
    return lax.dot_general(left, right, (((1,), (1,)), ((), ())), preferred_element_type=F32)


def inner_full(left, right):
    return lax.dot_general(
        left, right, (((1,), (1,)), ((), ())), precision=HIGHEST, preferred_element_type=F32
    )


def plain(left, right):
    return jnp.dot(left, right, preferred_element_type=F32)


def plain_full(left, right):
    return jnp.dot(left, right, precision=HIGHEST, preferred_element_type=F32)


def split(value):
    high = value.astype(BF16)
    return high, (value - high.astype(F32)).astype(BF16)


def three(product, left, right):
    return (
        product(left[0], right[1]) + product(left[1], right[0]) + product(left[0], right[0])
    )


def body(
    e_ref, v1_ref, v2_ref, t1_ref, t2_ref, out_ref,
    vbuf, vhigh, vlow, ebuf, obuf, t1, t2, nmat,
    psend, precv, zsend, zrecv, xbuf,
    gsend, grecv, gzrecv, gfull,
    loc_sem, own_sem,
    m1_s, m1_r, m2_s, m2_r, m3_s, m3_r, dd_s, dd_r, e_s, e_r,
    g_s, g_r, gz_s, gz_r, gp_s, gp_r,
    w_s, w_r, z_s, z_r, x_s, x_r, o_s, o_r,
):
    col = lax.axis_index("col")
    z = lax.axis_index("row")
    x, y, k = col // 8, (col // 2) % 4, col % 2
    ring = (x, y)
    cross = (y, x)

    def shift(at, by):
        return lax.rem(at + by, SIDE)

    def along_x(by):
        return (z, shift(x, by) * 8 + y * 2 + k)

    def along_y(by):
        return (z, x * 8 + shift(y, by) * 2 + k)

    def along_z(by):
        return (shift(z, by), col)

    partner = (z, x * 8 + y * 2 + (1 - k))
    ring_peer = (along_x, along_y)
    cross_peer = (along_y, along_x)

    sent = []

    def send(src, dst, s, r, device):
        copy = pltpu.make_async_remote_copy(
            src_ref=src, dst_ref=dst, send_sem=s, recv_sem=r, device_id=device, device_id_type=MESH
        )
        copy.start()
        sent.append(copy)
        return copy

    barrier = pltpu.get_barrier_semaphore()
    for by in OFFSETS:
        for peer in (along_x, along_y, along_z):
            pl.semaphore_signal(barrier, inc=1, device_id=peer(by), device_id_type=MESH)
    pl.semaphore_signal(barrier, inc=1, device_id=partner, device_id_type=MESH)

    local = []

    def bring(src, dst, sem):
        copy = pltpu.make_async_copy(src, dst, sem)
        copy.start()
        local.append(copy)
        return copy

    def columns(h, part):
        return pl.ds(pl.multiple_of(h * HALF + part * PART, PART), PART)

    panels = (v1_ref, v2_ref)
    own_v = [
        [bring(panels[p].at[:, columns(h, ring[h])], vbuf.at[h, p, x, y, k], loc_sem.at[2 * h + p]) for p in range(2)]
        for h in range(2)
    ]
    own_e = [bring(e_ref.at[:, columns(h, ring[h])], ebuf.at[h, ring[h]], loc_sem.at[4 + h]) for h in range(2)]
    own_t = [bring(t1_ref, t1, loc_sem.at[6]), bring(t2_ref, t2, loc_sem.at[7])]

    pl.semaphore_wait(barrier, 10)

    m1 = [[[None] * 2 for _ in OFFSETS] for _ in range(2)]
    for d, by in enumerate(OFFSETS):
        for h in range(2):
            for p in range(2):
                m1[h][d][p] = send(
                    panels[p].at[:, columns(h, shift(ring[h], by))],
                    vbuf.at[h, p, x, y, k],
                    m1_s.at[h, d, p], m1_r.at[h, d, p], ring_peer[h](by),
                )

    def chunk(h, p, at):
        return vbuf.at[h, p, :, at, k] if h == 0 else vbuf.at[h, p, at, :, k]

    m2 = [[[None] * 2 for _ in range(2)] for _ in range(2)]
    dd = [[], []]
    for h in range(2):
        for copy in own_v[h]:
            copy.wait()
        for d in range(3):
            for p in range(2):
                m1[h][d][p].wait_recv()
        for turn in range(2):
            for way, by in ((0, 1), (1, 3)):
                p = turn if way == 0 else 1 - turn
                m2[h][way][p] = send(
                    chunk(h, p, cross[h]), chunk(h, p, cross[h]), m2_s.at[h, way, p], m2_r.at[h, way, p], cross_peer[h](by)
                )
        for p in range(2):
            dd[h].append(send(chunk(h, p, cross[h]), chunk(h, p, cross[h]), dd_s.at[h, p], dd_r.at[h, p], partner))

    moved = [[None] * 3 for _ in range(2)]
    for d, by in enumerate(OFFSETS):
        for h in range(2):
            moved[h][d] = send(
                e_ref.at[:, columns(h, shift(ring[h], by))],
                ebuf.at[h, ring[h]],
                e_s.at[h, d], e_r.at[h, d], ring_peer[h](by),
            )

    m3 = [[None] * 2 for _ in range(2)]
    for turn in range(2):
        for h in range(2):
            for way, by in ((0, 1), (1, 3)):
                p = turn if way == 0 else 1 - turn
                came = shift(cross[h], 4 - by)
                m2[h][way][p].wait_recv()
                if turn == 0:
                    m3[h][way] = send(
                        chunk(h, p, came), chunk(h, p, came), m3_s.at[h, way], m3_r.at[h, way], cross_peer[h](by)
                    )
                at = 2 + 2 * way + p
                dd[h].append(send(chunk(h, p, came), chunk(h, p, came), dd_s.at[h, at], dd_r.at[h, at], partner))
    for h in range(2):
        far = shift(cross[h], 2)
        for way in range(2):
            m3[h][way].wait_recv()
            at = 6 + way
            dd[h].append(send(chunk(h, way, far), chunk(h, way, far), dd_s.at[h, at], dd_r.at[h, at], partner))

    for h in range(2):
        for copy in dd[h]:
            copy.wait_recv()

        def cut(i, carry):
            p, at_x, at_y = i // 16, (i // 4) % 4, i % 4
            rows = pl.ds(pl.multiple_of(i * 16, 16), 16)
            high, low = split(vbuf[h, p, at_x, at_y].reshape(16, PART))
            vhigh[h, rows, :] = high
            vlow[h, rows, :] = low
            return carry

        lax.fori_loop(0, 32, cut, 0)

    def vectors(h, p):
        rows = pl.ds(p * 256, 256)
        return vhigh[h, rows, :], vlow[h, rows, :]

    g = [[None] * 3 for _ in range(2)]
    for h in range(2):
        mine = vbuf[h, 0, :, y, k] if h == 0 else vbuf[h, 0, x, :, k]
        terms = three(inner, split(mine.reshape(32, PART)), vectors(h, 1))
        gsend[h] = terms.reshape(SIDE, 8, 256)
        for d, by in enumerate(OFFSETS):
            g[h][d] = send(
                gsend.at[h, shift(ring[h], by)], grecv.at[h, d], g_s.at[h, d], g_r.at[h, d], ring_peer[h](by)
            )
    total = gsend[0, x] + gsend[1, y]
    for h in range(2):
        for d in range(3):
            g[h][d].wait_recv()
            total = total + grecv[h, d]
    gzrecv[3] = total
    gz = [send(gzrecv.at[3], gzrecv.at[d], gz_s.at[d], gz_r.at[d], along_z(by)) for d, by in enumerate(OFFSETS)]
    for copy in gz:
        copy.wait_recv()
    gfull[x, y, k] = total + gzrecv[0] + gzrecv[1] + gzrecv[2]
    spread = [
        send(gfull.at[x, y, k], gfull.at[x, y, k], gp_s.at[d], gp_r.at[d], along_x(by)) for d, by in enumerate(OFFSETS)
    ]
    for copy in spread:
        copy.wait_recv()
    spread = [
        send(gfull.at[:, y, k], gfull.at[:, y, k], gp_s.at[3 + d], gp_r.at[3 + d], along_y(by))
        for d, by in enumerate(OFFSETS)
    ]
    for copy in spread:
        copy.wait_recv()
    send(gfull.at[:, :, k], gfull.at[:, :, k], gp_s.at[6], gp_r.at[6], partner).wait_recv()
    for copy in own_t:
        copy.wait()
    nmat[...] = plain_full(plain_full(t1[...], gfull[...].reshape(256, 256)), t2[...])

    w = [[None] * 3 for _ in range(2)]
    for h in range(2):
        own_e[h].wait()
        for d in range(3):
            moved[h][d].wait_recv()
        vecs = split(ebuf[h].reshape(SIDE * MINE, PART))
        for p in range(2):
            psend[h, :, :, pl.ds(p * 256, 256)] = three(inner, vecs, vectors(h, p)).reshape(SIDE, MINE, 256)
        for d, by in enumerate(OFFSETS):
            w[h][d] = send(
                psend.at[h, shift(ring[h], by)], precv.at[h, d], w_s.at[h, d], w_r.at[h, d], ring_peer[h](by)
            )
    total = psend[0, x] + psend[1, y]
    for h in range(2):
        for d in range(3):
            w[h][d].wait_recv()
            total = total + precv[h, d]
    zsend[...] = total
    zs = [send(zsend, zrecv.at[d], z_s.at[d], z_r.at[d], along_z(by)) for d, by in enumerate(OFFSETS)]
    for copy in zs:
        copy.wait_recv()
    total = total + zrecv[0] + zrecv[1] + zrecv[2]
    first, second = total[:, :256], total[:, 256:]
    coef_first = inner_full(first, t1[...]) - inner_full(second, nmat[...])
    coef_second = inner_full(second, t2[...])
    for h in range(2):
        xbuf[h, ring[h], :, pl.ds(0, 256)] = coef_first
        xbuf[h, ring[h], :, pl.ds(256, 256)] = coef_second
    xs = [[None] * 3 for _ in range(2)]
    for h in range(2):
        for d, by in enumerate(OFFSETS):
            xs[h][d] = send(
                xbuf.at[h, ring[h]], xbuf.at[h, ring[h]], x_s.at[h, d], x_r.at[h, d], ring_peer[h](by)
            )

    back = []
    for h in range(2):
        for d in range(3):
            xs[h][d].wait_recv()
        coefs = split(xbuf[h].reshape(SIDE * MINE, 512))
        for tile in range(PART // TILE):
            cols = pl.ds(tile * TILE, TILE)
            change = three(plain, coefs, (vhigh[h, :, cols], vlow[h, :, cols]))
            obuf[h, :, :, cols] = ebuf[h, :, :, cols] - change.reshape(SIDE, MINE, TILE)
            there = pl.ds(pl.multiple_of(h * HALF + ring[h] * PART + tile * TILE, TILE), TILE)
            for d, by in enumerate(OFFSETS):
                back.append(
                    send(
                        obuf.at[h, shift(ring[h], by), :, cols], out_ref.at[:, there],
                        o_s.at[h, tile, d], o_r.at[h, tile, d], ring_peer[h](by),
                    )
                )
            bring(obuf.at[h, ring[h], :, cols], out_ref.at[:, there], own_sem.at[h, tile]).wait()
    for copy in back:
        copy.wait_recv()
    for copy in sent:
        copy.wait_send()


def shards(evecs, v_first, v_second, t_first, t_second):
    vmem = pltpu.VMEM
    dma = pltpu.SemaphoreType.DMA
    tiles = PART // TILE

    def both(*shape):
        return [dma(shape), dma(shape)]

    return pl.pallas_call(
        body,
        out_shape=jax.ShapeDtypeStruct(evecs.shape, evecs.dtype),
        in_specs=[pl.BlockSpec(memory_space=pl.ANY)] * 5,
        out_specs=pl.BlockSpec(memory_space=pl.ANY),
        scratch_shapes=[
            vmem((2, 2, 4, 4, 2, 8, PART), F32),
            vmem((2, 512, PART), BF16),
            vmem((2, 512, PART), BF16),
            vmem((2, SIDE, MINE, PART), F32),
            vmem((2, SIDE, MINE, PART), F32),
            vmem((256, 256), F32),
            vmem((256, 256), F32),
            vmem((256, 256), F32),
            vmem((2, SIDE, MINE, 512), F32),
            vmem((2, 3, MINE, 512), F32),
            vmem((MINE, 512), F32),
            vmem((3, MINE, 512), F32),
            vmem((2, SIDE, MINE, 512), F32),
            vmem((2, SIDE, 8, 256), F32),
            vmem((2, 3, 8, 256), F32),
            vmem((4, 8, 256), F32),
            vmem((4, 4, 2, 8, 256), F32),
            dma((8,)),
            dma((2, tiles)),
            *both(2, 3, 2),
            *both(2, 2, 2),
            *both(2, 2),
            *both(2, 8),
            *both(2, 3),
            *both(2, 3),
            *both(3),
            *both(7),
            *both(2, 3),
            *both(3),
            *both(2, 3),
            *both(2, tiles, 3),
        ],
        compiler_params=pltpu.CompilerParams(
            collective_id=0, has_side_effects=True, vmem_limit_bytes=56 << 20
        ),
        name="back_transform",
    )(evecs, v_first, v_second, t_first, t_second)


def solution(mesh):
    placed = (P("col", "row"), P("col", "row"), P("col", "row"), P(), P())
    return jax.shard_map(
        shards, mesh=mesh, in_specs=placed, out_specs=P("col", "row"), check_vma=False
    )
```

```python
import jax
import jax.numpy as jnp
from jax import lax
from jax.experimental import pallas as pl
from jax.experimental.pallas import tpu as pltpu
from jax.sharding import PartitionSpec as P

MESH = pl.DeviceIdType.MESH
F32 = jnp.float32
BF16 = jnp.bfloat16
HIGHEST = lax.Precision.HIGHEST

SIDE = 4
HALF = 8192
PART = HALF // SIDE
MINE = 32
CHUNKS = 2
ROWS = MINE // CHUNKS
TILE = 1024
TILES = PART // TILE
OFFSETS = (1, 3, 2)
WAYS = ((0, 1), (1, 3))


def inner(left, right):
    return lax.dot_general(left, right, (((1,), (1,)), ((), ())), preferred_element_type=F32)


def inner_full(left, right):
    return lax.dot_general(
        left, right, (((1,), (1,)), ((), ())), precision=HIGHEST, preferred_element_type=F32
    )


def plain(left, right):
    return jnp.dot(left, right, preferred_element_type=F32)


def plain_full(left, right):
    return jnp.dot(left, right, precision=HIGHEST, preferred_element_type=F32)


def split(value):
    high = value.astype(BF16)
    return high, (value - high.astype(F32)).astype(BF16)


def products_of(vectors, rows):
    count = rows[0].shape[0]
    high = inner(vectors[0], jnp.concatenate(rows, axis=0))
    return (high[:, :count] + high[:, count:] + inner(vectors[1], rows[0])).T


def combine(coefs, vectors):
    count = coefs[0].shape[0]
    high = plain(jnp.concatenate(coefs, axis=0), vectors[0])
    return high[:count] + high[count:] + plain(coefs[0], vectors[1])


def body(
    e_ref, v1_ref, v2_ref, t1_ref, t2_ref, out_ref,
    vbuf, vhigh, vlow, ebuf, obuf, t1, t2, nmat,
    psend, precv, zsend, zrecv, xbuf,
    gsend, grecv, gpart, gfull,
    loc_sem, own_sem,
    m1_s, m1_r, m2_s, m2_r, m3_s, m3_r, dd_s, dd_r, e_s, e_r,
    g_s, g_r, gz_s, gz_r, gp_s, gp_r,
    w_s, w_r, z_s, z_r, x_s, x_r, o_s, o_r,
):
    col = lax.axis_index("col")
    z = lax.axis_index("row")
    x, y, k = col // 8, (col // 2) % 4, col % 2
    ring = (x, y)
    cross = (y, x)

    def shift(at, by):
        return lax.rem(at + by, SIDE)

    def device(dx=0, dy=0, dz=0, dk=0):
        return (shift(z, dz), shift(x, dx) * 8 + shift(y, dy) * 2 + lax.rem(k + dk, 2))

    def along_x(by):
        return device(dx=by)

    def along_y(by):
        return device(dy=by)

    def along_z(by):
        return device(dz=by)

    partner = device(dk=1)
    ring_peer = (along_x, along_y)
    cross_peer = (along_y, along_x)

    sent = []

    def send(src, dst, s, r, to):
        copy = pltpu.make_async_remote_copy(
            src_ref=src, dst_ref=dst, send_sem=s, recv_sem=r, device_id=to, device_id_type=MESH
        )
        copy.start()
        sent.append(copy)
        return copy

    barrier = pltpu.get_barrier_semaphore()
    row_peers = [(dx, dz) for dz in (0, *OFFSETS) for dx in (0, *OFFSETS) if dx or dz]
    col_peers = [(dy, dk) for dk in (0, 1) for dy in (0, *OFFSETS) if dy or dk]
    peers = [device(dx=dx, dz=dz) for dx, dz in row_peers] + [device(dy=dy, dk=dk) for dy, dk in col_peers]
    for peer in peers:
        pl.semaphore_signal(barrier, inc=1, device_id=peer, device_id_type=MESH)

    def bring(src, dst, sem):
        copy = pltpu.make_async_copy(src, dst, sem)
        copy.start()
        return copy

    def columns(h, part):
        return pl.ds(pl.multiple_of(h * HALF + part * PART, PART), PART)

    def rows(c):
        return pl.ds(c * ROWS, ROWS)

    panels = (v1_ref, v2_ref)
    both = range(2)
    own_v = [
        [bring(panels[p].at[:, columns(h, ring[h])], vbuf.at[h, p, x, y, k], loc_sem.at[2 * h + p]) for p in both]
        for h in both
    ]
    own_e = [
        [bring(e_ref.at[rows(c), columns(h, ring[h])], ebuf.at[h, c, ring[h]], loc_sem.at[4 + 2 * c + h]) for h in both]
        for c in range(CHUNKS)
    ]
    at_t = 4 + 2 * CHUNKS
    own_t = [bring(t1_ref, t1, loc_sem.at[at_t]), bring(t2_ref, t2, loc_sem.at[at_t + 1])]

    pl.semaphore_wait(barrier, len(peers))

    m1 = [[None] * 3 for _ in both]
    for d, by in enumerate(OFFSETS):
        for h in both:
            m1[h][d] = [
                send(
                    panels[p].at[:, columns(h, shift(ring[h], by))],
                    vbuf.at[h, p, x, y, k],
                    m1_s.at[h, d, p], m1_r.at[h, d, p], ring_peer[h](by),
                )
                for p in both
            ]

    def piece(h, j, at):
        origin = ring[h] if j == 0 else shift(ring[h], 4 - OFFSETS[j - 1])
        return vbuf.at[h, :, origin, at, k] if h == 0 else vbuf.at[h, :, at, origin, k]

    m2 = [[[None] * 4 for _ in both] for _ in both]
    m3 = [[[None] * 4 for _ in both] for _ in both]
    dd = [[None] * 20 for _ in both]

    def mirror(h, src, at):
        dd[h][at] = send(src, src, dd_s.at[h, at], dd_r.at[h, at], partner)

    def cut(h, j, at, copies):
        origin = ring[h] if j == 0 else shift(ring[h], 4 - OFFSETS[j - 1])
        at_x, at_y = (origin, at) if h == 0 else (at, origin)
        for copy in copies:
            dd[h][copy].wait_recv()
        for p in both:
            to = pl.ds(pl.multiple_of(p * 256 + at_x * 64 + at_y * 16, 16), 16)
            vhigh[h, to, :], vlow[h, to, :] = split(vbuf[h, p, at_x, at_y].reshape(16, PART))

    def pass_on(h, j):
        src = piece(h, j, cross[h])
        for way, by in WAYS:
            m2[h][way][j] = send(src, src, m2_s.at[h, way, j], m2_r.at[h, way, j], cross_peer[h](by))
        mirror(h, src, j)

    def pass_further(h, j):
        for way, by in WAYS:
            m2[h][way][j].wait_recv()
            src = piece(h, j, shift(cross[h], 4 - by))
            part = src.at[way]
            m3[h][way][j] = send(part, part, m3_s.at[h, way, j], m3_r.at[h, way, j], cross_peer[h](by))
            mirror(h, src, 4 + 4 * way + j)

    def finish(h, j):
        for way, _ in WAYS:
            m3[h][way][j].wait_recv()
            mirror(h, piece(h, j, shift(cross[h], 2)).at[way], 12 + 4 * way + j)

    def arrived(h, d):
        for p in both:
            m1[h][d][p].wait_recv()
        pass_on(h, d + 1)

    moved = [[[None] * 3 for _ in both] for _ in range(CHUNKS)]

    def move(c):
        for d, by in enumerate(OFFSETS):
            for h in both:
                moved[c][h][d] = send(
                    e_ref.at[rows(c), columns(h, shift(ring[h], by))],
                    ebuf.at[h, c, ring[h]],
                    e_s.at[c, h, d], e_r.at[c, h, d], ring_peer[h](by),
                )

    def cut_near(j):
        for h in both:
            cut(h, j, cross[h], [j])

    def cut_next(j):
        for h in both:
            for way, by in WAYS:
                cut(h, j, shift(cross[h], 4 - by), [4 + 4 * way + j])

    def cut_far(j):
        for h in both:
            cut(h, j, shift(cross[h], 2), [12 + j, 16 + j])

    for h in both:
        for copy in own_v[h]:
            copy.wait()
        pass_on(h, 0)
    for d in (0, 1):
        for h in both:
            arrived(h, d)
    for h in both:
        pass_further(h, 0)
    for h in both:
        arrived(h, 2)
    cut_near(0)
    cut_near(1)
    cut_near(2)
    for h in both:
        pass_further(h, 1)
    cut_near(3)
    for h in both:
        pass_further(h, 2)
    cut_next(0)
    cut_next(1)
    for h in both:
        pass_further(h, 3)
    move(0)
    move(1)
    for h in both:
        finish(h, 0)
    cut_next(2)
    for h in both:
        finish(h, 1)
    cut_next(3)
    for h in both:
        finish(h, 2)
    cut_far(0)
    for h in both:
        finish(h, 3)
    cut_far(1)
    cut_far(2)
    cut_far(3)

    g = [[None] * 3 for _ in both]
    for h in both:
        mine = vbuf[h, 0, :, y, k] if h == 0 else vbuf[h, 0, x, :, k]
        terms = products_of((vhigh[h, pl.ds(256, 256), :], vlow[h, pl.ds(256, 256), :]), split(mine.reshape(32, PART)))
        gsend[h] = terms.reshape(SIDE, 8, 256)
        for d, by in enumerate(OFFSETS):
            g[h][d] = send(
                gsend.at[h, shift(ring[h], by)], grecv.at[h, d], g_s.at[h, d], g_r.at[h, d], ring_peer[h](by)
            )

    def gram_rows():
        total = gsend[0, x] + gsend[1, y]
        for h in both:
            for d in range(3):
                g[h][d].wait_recv()
                total = total + grecv[h, d]
        gpart[z, x] = total
        mine = gpart.at[z, x]
        return [
            send(mine, mine, gz_s.at[i], gz_r.at[i], device(dx=dx, dz=dz)) for i, (dx, dz) in enumerate(row_peers)
        ]

    def gram_sum(copies):
        for copy in copies:
            copy.wait_recv()
        gfull[:, y, k] = gpart[0] + gpart[1] + gpart[2] + gpart[3]
        mine = gfull.at[:, y, k]
        return [
            send(mine, mine, gp_s.at[i], gp_r.at[i], device(dy=dy, dk=dk)) for i, (dy, dk) in enumerate(col_peers)
        ]

    def gram_use(copies):
        for copy in copies:
            copy.wait_recv()
        for copy in own_t:
            copy.wait()
        nmat[...] = plain_full(plain_full(t1[...], gfull[...].reshape(256, 256)), t2[...])

    w = [[[None] * 3 for _ in both] for _ in range(CHUNKS)]
    zs = [None] * CHUNKS
    xs = [[[None] * 3 for _ in both] for _ in range(CHUNKS)]
    back = []

    def products(c):
        for h in both:
            own_e[c][h].wait()
            for d in range(3):
                moved[c][h][d].wait_recv()
            vecs = split(ebuf[h, c].reshape(SIDE * ROWS, PART))
            psend[h, c] = products_of((vhigh[h], vlow[h]), vecs).reshape(SIDE, ROWS, 512)
            for d, by in enumerate(OFFSETS):
                w[c][h][d] = send(
                    psend.at[h, c, shift(ring[h], by)],
                    precv.at[c, h, d], w_s.at[c, h, d], w_r.at[c, h, d], ring_peer[h](by),
                )

    def plane_sum(c):
        total = psend[0, c, x] + psend[1, c, y]
        for h in both:
            for d in range(3):
                w[c][h][d].wait_recv()
                total = total + precv[c, h, d]
        zsend[c] = total
        zs[c] = [
            send(zsend.at[c], zrecv.at[c, d], z_s.at[c, d], z_r.at[c, d], along_z(by)) for d, by in enumerate(OFFSETS)
        ]

    def coefficients(c):
        total = zsend[c]
        for d in range(3):
            zs[c][d].wait_recv()
            total = total + zrecv[c, d]
        first, second = total[:, :256], total[:, 256:]
        coef_first = inner_full(first, t1[...]) - inner_full(second, nmat[...])
        coef_second = inner_full(second, t2[...])
        for h in both:
            xbuf[h, c, ring[h], :, pl.ds(0, 256)] = coef_first
            xbuf[h, c, ring[h], :, pl.ds(256, 256)] = coef_second
        for h in both:
            mine = xbuf.at[h, c, ring[h]]
            for d, by in enumerate(OFFSETS):
                xs[c][h][d] = send(mine, mine, x_s.at[c, h, d], x_r.at[c, h, d], ring_peer[h](by))

    def update(c):
        for h in both:
            for d in range(3):
                xs[c][h][d].wait_recv()
            coefs = split(xbuf[h, c].reshape(SIDE * ROWS, 512))
            for tile in range(TILES):
                cols = pl.ds(tile * TILE, TILE)
                change = combine(coefs, (vhigh[h, :, cols], vlow[h, :, cols]))
                obuf[h, c, :, :, cols] = ebuf[h, c, :, :, cols] - change.reshape(SIDE, ROWS, TILE)
                there = pl.ds(pl.multiple_of(h * HALF + ring[h] * PART + tile * TILE, TILE), TILE)
                for d, by in enumerate(OFFSETS):
                    back.append(
                        send(
                            obuf.at[h, c, shift(ring[h], by), :, cols], out_ref.at[rows(c), there],
                            o_s.at[c, h, tile, d], o_r.at[c, h, tile, d], ring_peer[h](by),
                        )
                    )
                stays.append(bring(obuf.at[h, c, ring[h], :, cols], out_ref.at[rows(c), there], own_sem.at[c, h, tile]))

    stays = []
    products(0)
    step = gram_rows()
    products(1)
    plane_sum(0)
    step = gram_sum(step)
    plane_sum(1)
    gram_use(step)
    coefficients(0)
    coefficients(1)
    update(0)
    update(1)
    for copy in back:
        copy.wait_recv()
    for copy in stays:
        copy.wait()
    for copy in sent:
        copy.wait_send()


def shards(evecs, v_first, v_second, t_first, t_second):
    vmem = pltpu.VMEM
    dma = pltpu.SemaphoreType.DMA

    def both(*shape):
        return [dma(shape), dma(shape)]

    return pl.pallas_call(
        body,
        out_shape=jax.ShapeDtypeStruct(evecs.shape, evecs.dtype),
        in_specs=[pl.BlockSpec(memory_space=pl.ANY)] * 5,
        out_specs=pl.BlockSpec(memory_space=pl.ANY),
        scratch_shapes=[
            vmem((2, 2, 4, 4, 2, 8, PART), F32),
            vmem((2, 512, PART), BF16),
            vmem((2, 512, PART), BF16),
            vmem((2, CHUNKS, SIDE, ROWS, PART), F32),
            vmem((2, CHUNKS, SIDE, ROWS, PART), F32),
            vmem((256, 256), F32),
            vmem((256, 256), F32),
            vmem((256, 256), F32),
            vmem((2, CHUNKS, SIDE, ROWS, 512), F32),
            vmem((CHUNKS, 2, 3, ROWS, 512), F32),
            vmem((CHUNKS, ROWS, 512), F32),
            vmem((CHUNKS, 3, ROWS, 512), F32),
            vmem((2, CHUNKS, SIDE, ROWS, 512), F32),
            vmem((2, SIDE, 8, 256), F32),
            vmem((2, 3, 8, 256), F32),
            vmem((4, 4, 8, 256), F32),
            vmem((4, 4, 2, 8, 256), F32),
            dma((6 + 2 * CHUNKS,)),
            dma((CHUNKS, 2, TILES)),
            *both(2, 3, 2),
            *both(2, 2, 4),
            *both(2, 2, 4),
            *both(2, 20),
            *both(CHUNKS, 2, 3),
            *both(2, 3),
            *both(15),
            *both(7),
            *both(CHUNKS, 2, 3),
            *both(CHUNKS, 3),
            *both(CHUNKS, 2, 3),
            *both(CHUNKS, 2, TILES, 3),
        ],
        compiler_params=pltpu.CompilerParams(
            collective_id=0, has_side_effects=True, vmem_limit_bytes=56 << 20
        ),
        name="back_transform",
    )(evecs, v_first, v_second, t_first, t_second)


def solution(mesh):
    placed = (P("col", "row"), P("col", "row"), P("col", "row"), P(), P())
    return jax.shard_map(
        shards, mesh=mesh, in_specs=placed, out_specs=P("col", "row"), check_vma=False
    )
```

```python
import jax
import jax.numpy as jnp
from jax import lax
from jax.experimental import pallas as pl
from jax.experimental.pallas import tpu as pltpu
from jax.sharding import PartitionSpec as P

MESH = pl.DeviceIdType.MESH
F32 = jnp.float32
BF16 = jnp.bfloat16
HIGHEST = lax.Precision.HIGHEST

SIDE = 4
HALF = 8192
PART = HALF // SIDE
MINE = 32
CHUNKS = 2
ROWS = MINE // CHUNKS
TILE = 1024
TILES = PART // TILE
OFFSETS = (1, 3, 2)
WAYS = ((0, 1), (1, 3))


def inner(left, right):
    return lax.dot_general(left, right, (((1,), (1,)), ((), ())), preferred_element_type=F32)


def inner_full(left, right):
    return lax.dot_general(
        left, right, (((1,), (1,)), ((), ())), precision=HIGHEST, preferred_element_type=F32
    )


def plain(left, right):
    return jnp.dot(left, right, preferred_element_type=F32)


def plain_full(left, right):
    return jnp.dot(left, right, precision=HIGHEST, preferred_element_type=F32)


def split(value):
    high = value.astype(BF16)
    return high, (value - high.astype(F32)).astype(BF16)


def products_of(vectors, rows):
    count = rows[0].shape[0]
    high = inner(vectors[0], jnp.concatenate(rows, axis=0))
    return high[:, :count] + high[:, count:] + inner(vectors[1], rows[0])


def combine(coefs, vectors):
    count = coefs[0].shape[0]
    high = plain(jnp.concatenate(coefs, axis=0), vectors[0])
    return high[:count] + high[count:] + plain(coefs[0], vectors[1])


def body(
    e_ref, v1_ref, v2_ref, t1_ref, t2_ref, out_ref,
    vbuf, vhigh, vlow, ebuf, obuf, t1, t2, t1_gram,
    psend, precv, zsend, zrecv, xbuf,
    gsend, grecv, gpart, gfull,
    loc_sem, own_sem,
    m1_s, m1_r, m2_s, m2_r, m3_s, m3_r, dd_s, dd_r, e_s, e_r,
    g_s, g_r, gz_s, gz_r, gp_s, gp_r,
    w_s, w_r, z_s, z_r, x_s, x_r, o_s, o_r,
):
    col = lax.axis_index("col")
    z = lax.axis_index("row")
    x, y, k = col // 8, (col // 2) % 4, col % 2
    ring = (x, y)
    cross = (y, x)

    def shift(at, by):
        return lax.rem(at + by, SIDE)

    def device(dx=0, dy=0, dz=0, dk=0):
        return (shift(z, dz), shift(x, dx) * 8 + shift(y, dy) * 2 + lax.rem(k + dk, 2))

    def along_x(by):
        return device(dx=by)

    def along_y(by):
        return device(dy=by)

    def along_z(by):
        return device(dz=by)

    partner = device(dk=1)
    ring_peer = (along_x, along_y)
    cross_peer = (along_y, along_x)

    sent = []

    def send(src, dst, s, r, to):
        copy = pltpu.make_async_remote_copy(
            src_ref=src, dst_ref=dst, send_sem=s, recv_sem=r, device_id=to, device_id_type=MESH
        )
        copy.start()
        sent.append(copy)
        return copy

    barrier = pltpu.get_barrier_semaphore()
    peers = [along(by) for along in (along_x, along_y, along_z) for by in OFFSETS] + [partner]
    for peer in peers:
        pl.semaphore_signal(barrier, inc=1, device_id=peer, device_id_type=MESH)

    def bring(src, dst, sem):
        copy = pltpu.make_async_copy(src, dst, sem)
        copy.start()
        return copy

    def columns(h, part):
        return pl.ds(pl.multiple_of(h * HALF + part * PART, PART), PART)

    def rows(c):
        return pl.ds(c * ROWS, ROWS)

    panels = (v1_ref, v2_ref)
    both = range(2)
    own_v = [
        [bring(panels[p].at[:, columns(h, ring[h])], vbuf.at[h, p, x, y, k], loc_sem.at[2 * h + p]) for p in both]
        for h in both
    ]
    own_e = [
        [bring(e_ref.at[rows(c), columns(h, ring[h])], ebuf.at[h, c, ring[h]], loc_sem.at[4 + 2 * c + h]) for h in both]
        for c in range(CHUNKS)
    ]
    at_t = 4 + 2 * CHUNKS
    own_t = [bring(t1_ref, t1, loc_sem.at[at_t]), bring(t2_ref, t2, loc_sem.at[at_t + 1])]

    pl.semaphore_wait(barrier, len(peers))

    m1 = [[None] * 3 for _ in both]
    for d, by in enumerate(OFFSETS):
        for h in both:
            m1[h][d] = [
                send(
                    panels[p].at[:, columns(h, shift(ring[h], by))],
                    vbuf.at[h, p, x, y, k],
                    m1_s.at[h, d, p], m1_r.at[h, d, p], ring_peer[h](by),
                )
                for p in both
            ]

    def piece(h, j, at):
        origin = ring[h] if j == 0 else shift(ring[h], 4 - OFFSETS[j - 1])
        return vbuf.at[h, :, origin, at, k] if h == 0 else vbuf.at[h, :, at, origin, k]

    m2 = [[[None] * 4 for _ in both] for _ in both]
    m3 = [[[None] * 4 for _ in both] for _ in both]
    dd = [[None] * 20 for _ in both]

    def mirror(h, src, at):
        dd[h][at] = send(src, src, dd_s.at[h, at], dd_r.at[h, at], partner)

    def cut(h, j, at, copies):
        origin = ring[h] if j == 0 else shift(ring[h], 4 - OFFSETS[j - 1])
        at_x, at_y = (origin, at) if h == 0 else (at, origin)
        for copy in copies:
            dd[h][copy].wait_recv()
        for p in both:
            to = pl.ds(pl.multiple_of(p * 256 + at_x * 64 + at_y * 16, 16), 16)
            vhigh[h, to, :], vlow[h, to, :] = split(vbuf[h, p, at_x, at_y].reshape(16, PART))

    def pass_on(h, j):
        src = piece(h, j, cross[h])
        for way, by in WAYS:
            m2[h][way][j] = send(src, src, m2_s.at[h, way, j], m2_r.at[h, way, j], cross_peer[h](by))
        mirror(h, src, j)

    def pass_further(h, j):
        for way, by in WAYS:
            m2[h][way][j].wait_recv()
            src = piece(h, j, shift(cross[h], 4 - by))
            part = src.at[way]
            m3[h][way][j] = send(part, part, m3_s.at[h, way, j], m3_r.at[h, way, j], cross_peer[h](by))
            mirror(h, src, 4 + 4 * way + j)

    def finish(h, j):
        for way, _ in WAYS:
            m3[h][way][j].wait_recv()
            mirror(h, piece(h, j, shift(cross[h], 2)).at[way], 12 + 4 * way + j)

    def arrived(h, d):
        for p in both:
            m1[h][d][p].wait_recv()
        pass_on(h, d + 1)

    moved = [[[None] * 3 for _ in both] for _ in range(CHUNKS)]

    def move(c):
        for d, by in enumerate(OFFSETS):
            for h in both:
                moved[c][h][d] = send(
                    e_ref.at[rows(c), columns(h, shift(ring[h], by))],
                    ebuf.at[h, c, ring[h]],
                    e_s.at[c, h, d], e_r.at[c, h, d], ring_peer[h](by),
                )

    def cut_near(j):
        for h in both:
            cut(h, j, cross[h], [j])

    def cut_next(j):
        for h in both:
            for way, by in WAYS:
                cut(h, j, shift(cross[h], 4 - by), [4 + 4 * way + j])

    def cut_far(j):
        for h in both:
            cut(h, j, shift(cross[h], 2), [12 + j, 16 + j])

    for h in both:
        for copy in own_v[h]:
            copy.wait()
        pass_on(h, 0)
    for d in (0, 1):
        for h in both:
            arrived(h, d)
    for h in both:
        pass_further(h, 0)
    for h in both:
        arrived(h, 2)
    cut_near(0)
    cut_near(1)
    cut_near(2)
    for h in both:
        pass_further(h, 1)
    cut_near(3)
    for h in both:
        pass_further(h, 2)
    cut_next(0)
    cut_next(1)
    for h in both:
        pass_further(h, 3)
    for h in both:
        finish(h, 0)
    move(0)
    cut_next(2)
    for h in both:
        finish(h, 1)
    cut_next(3)
    for h in both:
        finish(h, 2)
    cut_far(0)
    for h in both:
        finish(h, 3)
    cut_far(1)
    cut_far(2)
    cut_far(3)

    g = [[None] * 3 for _ in both]
    for h in both:
        mine = vbuf[h, 0, :, y, k] if h == 0 else vbuf[h, 0, x, :, k]
        terms = products_of((vhigh[h, pl.ds(256, 256), :], vlow[h, pl.ds(256, 256), :]), split(mine.reshape(32, PART)))
        gsend[h] = terms.T.reshape(SIDE, 8, 256)
        for d, by in enumerate(OFFSETS):
            g[h][d] = send(
                gsend.at[h, shift(ring[h], by)], grecv.at[h, d], g_s.at[h, d], g_r.at[h, d], ring_peer[h](by)
            )

    def gram_rows():
        total = gsend[0, x] + gsend[1, y]
        for h in both:
            for d in range(3):
                g[h][d].wait_recv()
                total = total + grecv[h, d]
        gpart[z, x] = total
        mine = gpart.at[z, x]
        return [send(mine, mine, gz_s.at[d], gz_r.at[d], along_z(by)) for d, by in enumerate(OFFSETS)]

    def gram_spread(copies):
        for copy in copies:
            copy.wait_recv()
        gfull[x, y, k] = gpart[0, x] + gpart[1, x] + gpart[2, x] + gpart[3, x]
        mine = gfull.at[x, y, k]
        return [send(mine, mine, gz_s.at[3 + d], gz_r.at[3 + d], along_x(by)) for d, by in enumerate(OFFSETS)]

    def gram_sum(copies):
        for copy in copies:
            copy.wait_recv()
        mine = gfull.at[:, y, k]
        return [send(mine, mine, gp_s.at[d], gp_r.at[d], along_y(by)) for d, by in enumerate(OFFSETS)]

    def gram_partner(copies):
        for copy in copies:
            copy.wait_recv()
        mine = gfull.at[:, :, k]
        return [send(mine, mine, gp_s.at[3], gp_r.at[3], partner)]

    def gram_use(copies):
        for copy in copies:
            copy.wait_recv()
        t1_gram[...] = plain_full(t1[...], gfull[...].reshape(256, 256))

    w = [[[None] * 3 for _ in both] for _ in range(CHUNKS)]
    zs = [None] * CHUNKS
    xs = [[[None] * 3 for _ in both] for _ in range(CHUNKS)]
    back = []

    def products(c):
        terms = []
        for h in both:
            own_e[c][h].wait()
            for d in range(3):
                moved[c][h][d].wait_recv()
            vecs = split(ebuf[h, c].reshape(SIDE * ROWS, PART))
            terms.append(products_of((vhigh[h], vlow[h]), vecs))
        psend[:, c] = jnp.concatenate(terms, axis=1).T.reshape(2, SIDE, ROWS, 512)
        for h in both:
            for d, by in enumerate(OFFSETS):
                w[c][h][d] = send(
                    psend.at[h, c, shift(ring[h], by)],
                    precv.at[c, h, d], w_s.at[c, h, d], w_r.at[c, h, d], ring_peer[h](by),
                )

    def plane_sum(c):
        total = psend[0, c, x] + psend[1, c, y]
        for h in both:
            for d in range(3):
                w[c][h][d].wait_recv()
                total = total + precv[c, h, d]
        zsend[c] = total
        zs[c] = [
            send(zsend.at[c], zrecv.at[c, d], z_s.at[c, d], z_r.at[c, d], along_z(by)) for d, by in enumerate(OFFSETS)
        ]

    def coefficients(c):
        total = zsend[c]
        for copy in own_t if c == 0 else []:
            copy.wait()
        for d in range(3):
            zs[c][d].wait_recv()
            total = total + zrecv[c, d]
        first, second = total[:, :256], total[:, 256:]
        coef_second = inner_full(second, t2[...])
        coef_first = inner_full(first, t1[...])
        for h in both:
            xbuf[h, c, ring[h], :, pl.ds(0, 256)] = coef_first
            xbuf[h, c, ring[h], :, pl.ds(256, 256)] = coef_second
        for h in both:
            mine = xbuf.at[h, c, ring[h]]
            for d, by in enumerate(OFFSETS):
                xs[c][h][d] = send(mine, mine, x_s.at[c, h, d], x_r.at[c, h, d], ring_peer[h](by))

    def update(c):
        for h in both:
            for d in range(3):
                xs[c][h][d].wait_recv()
            first, second = (xbuf[h, c, :, :, pl.ds(p * 256, 256)].reshape(SIDE * ROWS, 256) for p in both)
            first = first - inner_full(second, t1_gram[...])
            coefs = split(jnp.concatenate([first, second], axis=1))
            for tile in range(TILES):
                cols = pl.ds(tile * TILE, TILE)
                change = combine(coefs, (vhigh[h, :, cols], vlow[h, :, cols]))
                obuf[h, c, :, :, cols] = ebuf[h, c, :, :, cols] - change.reshape(SIDE, ROWS, TILE)
                there = pl.ds(pl.multiple_of(h * HALF + ring[h] * PART + tile * TILE, TILE), TILE)
                for d, by in enumerate(OFFSETS):
                    back.append(
                        send(
                            obuf.at[h, c, shift(ring[h], by), :, cols], out_ref.at[rows(c), there],
                            o_s.at[c, h, tile, d], o_r.at[c, h, tile, d], ring_peer[h](by),
                        )
                    )
                stays.append(bring(obuf.at[h, c, ring[h], :, cols], out_ref.at[rows(c), there], own_sem.at[c, h, tile]))

    stays = []
    move(1)
    products(0)
    step = gram_rows()
    plane_sum(0)
    step = gram_spread(step)
    products(1)
    step = gram_sum(step)
    coefficients(0)
    plane_sum(1)
    step = gram_partner(step)
    gram_use(step)
    coefficients(1)
    update(0)
    update(1)
    for copy in back:
        copy.wait_recv()
    for copy in stays:
        copy.wait()
    for copy in sent:
        copy.wait_send()


def hand_over(src, dst, held, sems):
    spots = [(pl.ds(i * 8, 8), pl.ds(j * 8192, 8192)) for i in range(4) for j in range(2)]
    arriving = [pltpu.make_async_copy(src.at[spot], held.at[spot], sems.at[0, i]) for i, spot in enumerate(spots)]
    leaving = [pltpu.make_async_copy(held.at[spot], dst.at[spot], sems.at[1, i]) for i, spot in enumerate(spots)]
    for copy in arriving:
        copy.start()
    for came, copy in zip(arriving, leaving):
        came.wait()
        copy.start()
    for copy in leaving:
        copy.wait()


def shards(evecs, v_first, v_second, t_first, t_second):
    vmem = pltpu.VMEM
    dma = pltpu.SemaphoreType.DMA

    def both(*shape):
        return [dma(shape), dma(shape)]

    basis = pl.pallas_call(
        body,
        out_shape=jax.ShapeDtypeStruct(evecs.shape, evecs.dtype),
        in_specs=[pl.BlockSpec(memory_space=pl.ANY)] * 5,
        out_specs=pl.BlockSpec(memory_space=pl.ANY),
        scratch_shapes=[
            vmem((2, 2, 4, 4, 2, 8, PART), F32),
            vmem((2, 512, PART), BF16),
            vmem((2, 512, PART), BF16),
            vmem((2, CHUNKS, SIDE, ROWS, PART), F32),
            vmem((2, CHUNKS, SIDE, ROWS, PART), F32),
            vmem((256, 256), F32),
            vmem((256, 256), F32),
            vmem((256, 256), F32),
            vmem((2, CHUNKS, SIDE, ROWS, 512), F32),
            vmem((CHUNKS, 2, 3, ROWS, 512), F32),
            vmem((CHUNKS, ROWS, 512), F32),
            vmem((CHUNKS, 3, ROWS, 512), F32),
            vmem((2, CHUNKS, SIDE, ROWS, 512), F32),
            vmem((2, SIDE, 8, 256), F32),
            vmem((2, 3, 8, 256), F32),
            vmem((4, 4, 8, 256), F32),
            vmem((4, 4, 2, 8, 256), F32),
            dma((6 + 2 * CHUNKS,)),
            dma((CHUNKS, 2, TILES)),
            *both(2, 3, 2),
            *both(2, 2, 4),
            *both(2, 2, 4),
            *both(2, 20),
            *both(CHUNKS, 2, 3),
            *both(2, 3),
            *both(6),
            *both(4),
            *both(CHUNKS, 2, 3),
            *both(CHUNKS, 3),
            *both(CHUNKS, 2, 3),
            *both(CHUNKS, 2, TILES, 3),
        ],
        compiler_params=pltpu.CompilerParams(
            collective_id=0, has_side_effects=True, vmem_limit_bytes=56 << 20
        ),
        name="back_transform",
    )(evecs, v_first, v_second, t_first, t_second)
    return pl.pallas_call(
        hand_over,
        out_shape=jax.ShapeDtypeStruct(evecs.shape, evecs.dtype),
        in_specs=[pl.BlockSpec(memory_space=pl.ANY)],
        out_specs=pl.BlockSpec(memory_space=pl.ANY),
        scratch_shapes=[vmem(evecs.shape, F32), dma((2, 8))],
        compiler_params=pltpu.CompilerParams(vmem_limit_bytes=56 << 20),
        name="hand_over",
    )(basis)


def solution(mesh):
    placed = (P("col", "row"), P("col", "row"), P("col", "row"), P(), P())
    return jax.shard_map(
        shards, mesh=mesh, in_specs=placed, out_specs=P("col", "row"), check_vma=False
    )
```

```python
import jax
import jax.numpy as jnp
from jax import lax
from jax.experimental import pallas as pl
from jax.experimental.pallas import tpu as pltpu
from jax.sharding import PartitionSpec as P

MESH = pl.DeviceIdType.MESH
F32 = jnp.float32
BF16 = jnp.bfloat16
HIGHEST = lax.Precision.HIGHEST

SIDE = 4
HALF = 8192
PART = HALF // SIDE
MINE = 32
SIZES = (16, 16)
STARTS = tuple(sum(SIZES[:c]) for c in range(len(SIZES)))
CHUNKS = len(SIZES)
TILE = 1024
TILES = PART // TILE
OFFSETS = (1, 3, 2)
WAYS = ((0, 1), (1, 3))


def inner(left, right):
    return lax.dot_general(left, right, (((1,), (1,)), ((), ())), preferred_element_type=F32)


def inner_full(left, right):
    return lax.dot_general(
        left, right, (((1,), (1,)), ((), ())), precision=HIGHEST, preferred_element_type=F32
    )


def plain(left, right):
    return jnp.dot(left, right, preferred_element_type=F32)


def plain_full(left, right):
    return jnp.dot(left, right, precision=HIGHEST, preferred_element_type=F32)


def split(value):
    high = value.astype(BF16)
    return high, (value - high.astype(F32)).astype(BF16)


def products_of(vectors, rows):
    count = rows[0].shape[0]
    high = inner(vectors[0], jnp.concatenate(rows, axis=0))
    return high[:, :count] + high[:, count:] + inner(vectors[1], rows[0])


def combine(coefs, vectors):
    count = coefs[0].shape[0]
    high = plain(jnp.concatenate(coefs, axis=0), vectors[0])
    return high[:count] + high[count:] + plain(coefs[0], vectors[1])


def body(
    e_ref, v1_ref, v2_ref, t1_ref, t2_ref, out_ref,
    vbuf, vhigh, vlow, ebuf, obuf, t1, t2, t1_gram,
    psend, precv, zsend, zrecv, xbuf,
    gsend, grecv, gpart, gfull,
    loc_sem, own_sem,
    m1_s, m1_r, m2_s, m2_r, m3_s, m3_r, dd_s, dd_r, e_s, e_r,
    g_s, g_r, gz_s, gz_r, gp_s, gp_r,
    w_s, w_r, z_s, z_r, x_s, x_r, o_s, o_r,
):
    col = lax.axis_index("col")
    z = lax.axis_index("row")
    x, y, k = col // 8, (col // 2) % 4, col % 2
    ring = (x, y)
    cross = (y, x)

    def shift(at, by):
        return lax.rem(at + by, SIDE)

    def device(dx=0, dy=0, dz=0, dk=0):
        return (shift(z, dz), shift(x, dx) * 8 + shift(y, dy) * 2 + lax.rem(k + dk, 2))

    def along_x(by):
        return device(dx=by)

    def along_y(by):
        return device(dy=by)

    def along_z(by):
        return device(dz=by)

    partner = device(dk=1)
    ring_peer = (along_x, along_y)
    cross_peer = (along_y, along_x)

    sent = []

    def send(src, dst, s, r, to):
        copy = pltpu.make_async_remote_copy(
            src_ref=src, dst_ref=dst, send_sem=s, recv_sem=r, device_id=to, device_id_type=MESH
        )
        copy.start()
        sent.append(copy)
        return copy

    barrier = pltpu.get_barrier_semaphore()
    peers = [along(by) for along in (along_x, along_y, along_z) for by in OFFSETS] + [partner]
    for peer in peers:
        pl.semaphore_signal(barrier, inc=1, device_id=peer, device_id_type=MESH)

    def bring(src, dst, sem):
        copy = pltpu.make_async_copy(src, dst, sem)
        copy.start()
        return copy

    def columns(h, part):
        return pl.ds(pl.multiple_of(h * HALF + part * PART, PART), PART)

    def rows(c):
        return pl.ds(STARTS[c], SIZES[c])

    panels = (v1_ref, v2_ref)
    both = range(2)
    own_v = [
        [bring(panels[p].at[:, columns(h, ring[h])], vbuf.at[h, p, x, y, k], loc_sem.at[2 * h + p]) for p in both]
        for h in both
    ]
    own_e = [
        [bring(e_ref.at[rows(c), columns(h, ring[h])], ebuf.at[h, ring[h], rows(c)], loc_sem.at[4 + 2 * c + h]) for h in both]
        for c in range(CHUNKS)
    ]
    at_t = 4 + 2 * CHUNKS
    own_t = [bring(t1_ref, t1, loc_sem.at[at_t]), bring(t2_ref, t2, loc_sem.at[at_t + 1])]

    pl.semaphore_wait(barrier, len(peers))

    m1 = [[None] * 3 for _ in both]
    for d, by in enumerate(OFFSETS):
        for h in both:
            m1[h][d] = [
                send(
                    panels[p].at[:, columns(h, shift(ring[h], by))],
                    vbuf.at[h, p, x, y, k],
                    m1_s.at[h, d, p], m1_r.at[h, d, p], ring_peer[h](by),
                )
                for p in both
            ]

    def piece(h, j, at):
        origin = ring[h] if j == 0 else shift(ring[h], 4 - OFFSETS[j - 1])
        return vbuf.at[h, :, origin, at, k] if h == 0 else vbuf.at[h, :, at, origin, k]

    m2 = [[[None] * 4 for _ in both] for _ in both]
    m3 = [[[None] * 4 for _ in both] for _ in both]
    dd = [[None] * 20 for _ in both]

    def mirror(h, src, at):
        dd[h][at] = send(src, src, dd_s.at[h, at], dd_r.at[h, at], partner)

    def cut(h, j, at, copies):
        origin = ring[h] if j == 0 else shift(ring[h], 4 - OFFSETS[j - 1])
        at_x, at_y = (origin, at) if h == 0 else (at, origin)
        for copy in copies:
            dd[h][copy].wait_recv()
        for p in both:
            to = pl.ds(pl.multiple_of(p * 256 + at_x * 64 + at_y * 16, 16), 16)
            vhigh[h, to, :], vlow[h, to, :] = split(vbuf[h, p, at_x, at_y].reshape(16, PART))

    def pass_on(h, j):
        src = piece(h, j, cross[h])
        for way, by in WAYS:
            m2[h][way][j] = send(src, src, m2_s.at[h, way, j], m2_r.at[h, way, j], cross_peer[h](by))
        mirror(h, src, j)

    def pass_further(h, j):
        for way, by in WAYS:
            m2[h][way][j].wait_recv()
            src = piece(h, j, shift(cross[h], 4 - by))
            part = src.at[way]
            m3[h][way][j] = send(part, part, m3_s.at[h, way, j], m3_r.at[h, way, j], cross_peer[h](by))
            mirror(h, src, 4 + 4 * way + j)

    def finish(h, j):
        for way, _ in WAYS:
            m3[h][way][j].wait_recv()
            mirror(h, piece(h, j, shift(cross[h], 2)).at[way], 12 + 4 * way + j)

    def arrived(h, d):
        for p in both:
            m1[h][d][p].wait_recv()
        pass_on(h, d + 1)

    moved = [[[None] * 3 for _ in both] for _ in range(CHUNKS)]

    def move(c):
        for d, by in enumerate(OFFSETS):
            for h in both:
                moved[c][h][d] = send(
                    e_ref.at[rows(c), columns(h, shift(ring[h], by))],
                    ebuf.at[h, ring[h], rows(c)],
                    e_s.at[c, h, d], e_r.at[c, h, d], ring_peer[h](by),
                )

    def cut_near(j):
        for h in both:
            cut(h, j, cross[h], [j])

    def cut_next(j):
        for h in both:
            for way, by in WAYS:
                cut(h, j, shift(cross[h], 4 - by), [4 + 4 * way + j])

    def cut_far(j):
        for h in both:
            cut(h, j, shift(cross[h], 2), [12 + j, 16 + j])

    for h in both:
        for copy in own_v[h]:
            copy.wait()
        pass_on(h, 0)
    for d in (0, 1):
        for h in both:
            arrived(h, d)
    for h in both:
        pass_further(h, 0)
    for h in both:
        arrived(h, 2)
    cut_near(0)
    cut_near(1)
    cut_near(2)
    for h in both:
        pass_further(h, 1)
    cut_near(3)
    for h in both:
        pass_further(h, 2)
    cut_next(0)
    cut_next(1)
    for h in both:
        pass_further(h, 3)
    for h in both:
        finish(h, 0)
    move(0)
    cut_next(2)
    for h in both:
        finish(h, 1)
    cut_next(3)
    for h in both:
        finish(h, 2)
    cut_far(0)
    for h in both:
        finish(h, 3)
    cut_far(1)
    cut_far(2)
    cut_far(3)

    g = [[None] * 3 for _ in both]
    for h in both:
        mine = vbuf[h, 0, :, y, k] if h == 0 else vbuf[h, 0, x, :, k]
        terms = products_of((vhigh[h, pl.ds(256, 256), :], vlow[h, pl.ds(256, 256), :]), split(mine.reshape(32, PART)))
        gsend[h] = terms.T.reshape(SIDE, 8, 256)
        for d, by in enumerate(OFFSETS):
            g[h][d] = send(
                gsend.at[h, shift(ring[h], by)], grecv.at[h, d], g_s.at[h, d], g_r.at[h, d], ring_peer[h](by)
            )

    def gram_rows():
        total = gsend[0, x] + gsend[1, y]
        for h in both:
            for d in range(3):
                g[h][d].wait_recv()
                total = total + grecv[h, d]
        gpart[z, x] = total
        mine = gpart.at[z, x]
        return [send(mine, mine, gz_s.at[d], gz_r.at[d], along_z(by)) for d, by in enumerate(OFFSETS)]

    def gram_spread(copies):
        for copy in copies:
            copy.wait_recv()
        gfull[x, y, k] = gpart[0, x] + gpart[1, x] + gpart[2, x] + gpart[3, x]
        mine = gfull.at[x, y, k]
        return [send(mine, mine, gz_s.at[3 + d], gz_r.at[3 + d], along_x(by)) for d, by in enumerate(OFFSETS)]

    def gram_sum(copies):
        for copy in copies:
            copy.wait_recv()
        mine = gfull.at[:, y, k]
        return [send(mine, mine, gp_s.at[d], gp_r.at[d], along_y(by)) for d, by in enumerate(OFFSETS)]

    def gram_partner(copies):
        for copy in copies:
            copy.wait_recv()
        mine = gfull.at[:, :, k]
        return [send(mine, mine, gp_s.at[3], gp_r.at[3], partner)]

    def gram_use(copies):
        for copy in copies:
            copy.wait_recv()
        t1_gram[...] = plain_full(t1[...], gfull[...].reshape(256, 256))

    w = [[[None] * 3 for _ in both] for _ in range(CHUNKS)]
    zs = [None] * CHUNKS
    xs = [[[None] * 3 for _ in both] for _ in range(CHUNKS)]
    back = []

    def products(c):
        terms = []
        for h in both:
            own_e[c][h].wait()
            for d in range(3):
                moved[c][h][d].wait_recv()
            vecs = split(ebuf[h, :, rows(c), :].reshape(SIDE * SIZES[c], PART))
            terms.append(products_of((vhigh[h], vlow[h]), vecs))
        psend[:, :, rows(c), :] = jnp.concatenate(terms, axis=1).T.reshape(2, SIDE, SIZES[c], 512)
        for h in both:
            for d, by in enumerate(OFFSETS):
                w[c][h][d] = send(
                    psend.at[h, shift(ring[h], by), rows(c)],
                    precv.at[h, d, rows(c)], w_s.at[c, h, d], w_r.at[c, h, d], ring_peer[h](by),
                )

    def plane_sum(c):
        total = psend[0, x, rows(c), :] + psend[1, y, rows(c), :]
        for h in both:
            for d in range(3):
                w[c][h][d].wait_recv()
                total = total + precv[h, d, rows(c), :]
        zsend[rows(c), :] = total
        zs[c] = [
            send(zsend.at[rows(c)], zrecv.at[d, rows(c)], z_s.at[c, d], z_r.at[c, d], along_z(by)) for d, by in enumerate(OFFSETS)
        ]

    def coefficients(c):
        total = zsend[rows(c), :]
        for copy in own_t if c == 0 else []:
            copy.wait()
        for d in range(3):
            zs[c][d].wait_recv()
            total = total + zrecv[d, rows(c), :]
        first, second = total[:, :256], total[:, 256:]
        coef_second = inner_full(second, t2[...])
        coef_first = inner_full(first, t1[...])
        for h in both:
            xbuf[h, ring[h], rows(c), pl.ds(0, 256)] = coef_first
            xbuf[h, ring[h], rows(c), pl.ds(256, 256)] = coef_second
        for h in both:
            mine = xbuf.at[h, ring[h], rows(c)]
            for d, by in enumerate(OFFSETS):
                xs[c][h][d] = send(mine, mine, x_s.at[c, h, d], x_r.at[c, h, d], ring_peer[h](by))

    def update(c):
        count = SIDE * SIZES[c]
        for h in both:
            for d in range(3):
                xs[c][h][d].wait_recv()
        first, second = (xbuf[:, :, rows(c), pl.ds(p * 256, 256)].reshape(2 * count, 256) for p in both)
        first = first - inner_full(second, t1_gram[...])
        high, low = split(jnp.concatenate([first, second], axis=1))
        for tile in range(TILES):
            cols = pl.ds(tile * TILE, TILE)
            for h in both:
                coefs = (high[h * count : (h + 1) * count], low[h * count : (h + 1) * count])
                change = combine(coefs, (vhigh[h, :, cols], vlow[h, :, cols]))
                obuf[h, :, rows(c), cols] = ebuf[h, :, rows(c), cols] - change.reshape(SIDE, SIZES[c], TILE)
                there = pl.ds(pl.multiple_of(h * HALF + ring[h] * PART + tile * TILE, TILE), TILE)
                for d, by in enumerate(OFFSETS):
                    back.append(
                        send(
                            obuf.at[h, shift(ring[h], by), rows(c), cols], out_ref.at[rows(c), there],
                            o_s.at[c, h, tile, d], o_r.at[c, h, tile, d], ring_peer[h](by),
                        )
                    )
                stays.append(bring(obuf.at[h, ring[h], rows(c), cols], out_ref.at[rows(c), there], own_sem.at[c, h, tile]))

    stays = []
    move(1)
    products(0)
    step = gram_rows()
    plane_sum(0)
    step = gram_spread(step)
    products(1)
    step = gram_sum(step)
    coefficients(0)
    plane_sum(1)
    step = gram_partner(step)
    gram_use(step)
    coefficients(1)
    update(0)
    update(1)
    for copy in back:
        copy.wait_recv()
    for copy in stays:
        copy.wait()
    for copy in sent:
        copy.wait_send()


def hand_over(src, dst, held, sems):
    spots = [(pl.ds(i * 8, 8), pl.ds(j * 8192, 8192)) for i in range(4) for j in range(2)]
    arriving = [pltpu.make_async_copy(src.at[spot], held.at[spot], sems.at[0, i]) for i, spot in enumerate(spots)]
    leaving = [pltpu.make_async_copy(held.at[spot], dst.at[spot], sems.at[1, i]) for i, spot in enumerate(spots)]
    for copy in arriving:
        copy.start()
    for came, copy in zip(arriving, leaving):
        came.wait()
        copy.start()
    for copy in leaving:
        copy.wait()


def shards(evecs, v_first, v_second, t_first, t_second):
    vmem = pltpu.VMEM
    dma = pltpu.SemaphoreType.DMA

    def both(*shape):
        return [dma(shape), dma(shape)]

    basis = pl.pallas_call(
        body,
        out_shape=jax.ShapeDtypeStruct(evecs.shape, evecs.dtype),
        in_specs=[pl.BlockSpec(memory_space=pl.ANY)] * 5,
        out_specs=pl.BlockSpec(memory_space=pl.ANY),
        scratch_shapes=[
            vmem((2, 2, 4, 4, 2, 8, PART), F32),
            vmem((2, 512, PART), BF16),
            vmem((2, 512, PART), BF16),
            vmem((2, SIDE, MINE, PART), F32),
            vmem((2, SIDE, MINE, PART), F32),
            vmem((256, 256), F32),
            vmem((256, 256), F32),
            vmem((256, 256), F32),
            vmem((2, SIDE, MINE, 512), F32),
            vmem((2, 3, MINE, 512), F32),
            vmem((MINE, 512), F32),
            vmem((3, MINE, 512), F32),
            vmem((2, SIDE, MINE, 512), F32),
            vmem((2, SIDE, 8, 256), F32),
            vmem((2, 3, 8, 256), F32),
            vmem((4, 4, 8, 256), F32),
            vmem((4, 4, 2, 8, 256), F32),
            dma((6 + 2 * CHUNKS,)),
            dma((CHUNKS, 2, TILES)),
            *both(2, 3, 2),
            *both(2, 2, 4),
            *both(2, 2, 4),
            *both(2, 20),
            *both(CHUNKS, 2, 3),
            *both(2, 3),
            *both(6),
            *both(4),
            *both(CHUNKS, 2, 3),
            *both(CHUNKS, 3),
            *both(CHUNKS, 2, 3),
            *both(CHUNKS, 2, TILES, 3),
        ],
        compiler_params=pltpu.CompilerParams(
            collective_id=0, has_side_effects=True, vmem_limit_bytes=56 << 20
        ),
        name="back_transform",
    )(evecs, v_first, v_second, t_first, t_second)
    return pl.pallas_call(
        hand_over,
        out_shape=jax.ShapeDtypeStruct(evecs.shape, evecs.dtype),
        in_specs=[pl.BlockSpec(memory_space=pl.ANY)],
        out_specs=pl.BlockSpec(memory_space=pl.ANY),
        scratch_shapes=[vmem(evecs.shape, F32), dma((2, 8))],
        compiler_params=pltpu.CompilerParams(vmem_limit_bytes=56 << 20),
        name="hand_over",
    )(basis)


def solution(mesh):
    placed = (P("col", "row"), P("col", "row"), P("col", "row"), P(), P())
    return jax.shard_map(
        shards, mesh=mesh, in_specs=placed, out_specs=P("col", "row"), check_vma=False
    )
```

```python
import jax
import jax.numpy as jnp
from jax import lax
from jax.experimental import pallas as pl
from jax.experimental.pallas import tpu as pltpu
from jax.sharding import PartitionSpec as P

MESH = pl.DeviceIdType.MESH
F32 = jnp.float32
BF16 = jnp.bfloat16
HIGHEST = lax.Precision.HIGHEST

SIDE = 4
HALF = 8192
PART = HALF // SIDE
MINE = 32
SIZES = (16, 16)
STARTS = tuple(sum(SIZES[:c]) for c in range(len(SIZES)))
CHUNKS = len(SIZES)
TILE = 1024
TILES = PART // TILE
OFFSETS = (1, 3, 2)
WAYS = ((0, 1), (1, 3))


def inner(left, right):
    return lax.dot_general(left, right, (((1,), (1,)), ((), ())), preferred_element_type=F32)


def inner_full(left, right):
    return lax.dot_general(
        left, right, (((1,), (1,)), ((), ())), precision=HIGHEST, preferred_element_type=F32
    )


def plain(left, right):
    return jnp.dot(left, right, preferred_element_type=F32)


def plain_full(left, right):
    return jnp.dot(left, right, precision=HIGHEST, preferred_element_type=F32)


def split(value):
    high = value.astype(BF16)
    return high, (value - high.astype(F32)).astype(BF16)


def products_of(vectors, rows):
    count = rows[0].shape[0]
    high = inner(vectors[0], jnp.concatenate(rows, axis=0))
    return high[:, :count] + high[:, count:] + inner(vectors[1], rows[0])


def combine(coefs, vectors):
    count = coefs[0].shape[0]
    high = plain(jnp.concatenate(coefs, axis=0), vectors[0])
    return high[:count] + high[count:] + plain(coefs[0], vectors[1])


def body(
    e_ref, v1_ref, v2_ref, t1_ref, t2_ref, out_ref,
    vbuf, vhigh, vlow, ebuf, obuf, t1, t2, t1_gram,
    psend, precv, zsend, zrecv, xbuf,
    gsend, grecv, gpart, gfull,
    loc_sem, own_sem,
    m1_s, m1_r, m2_s, m2_r, m3_s, m3_r, dd_s, dd_r, e_s, e_r,
    g_s, g_r, gz_s, gz_r, gp_s, gp_r,
    w_s, w_r, z_s, z_r, x_s, x_r, o_s, o_r,
):
    col = lax.axis_index("col")
    z = lax.axis_index("row")
    x, y, k = col // 8, (col // 2) % 4, col % 2
    ring = (x, y)
    cross = (y, x)

    def shift(at, by):
        return lax.rem(at + by, SIDE)

    def device(dx=0, dy=0, dz=0, dk=0):
        return (shift(z, dz), shift(x, dx) * 8 + shift(y, dy) * 2 + lax.rem(k + dk, 2))

    def along_x(by):
        return device(dx=by)

    def along_y(by):
        return device(dy=by)

    def along_z(by):
        return device(dz=by)

    partner = device(dk=1)
    ring_peer = (along_x, along_y)
    cross_peer = (along_y, along_x)

    sent = []

    def send(src, dst, s, r, to):
        copy = pltpu.make_async_remote_copy(
            src_ref=src, dst_ref=dst, send_sem=s, recv_sem=r, device_id=to, device_id_type=MESH
        )
        copy.start()
        sent.append(copy)
        return copy

    barrier = pltpu.get_barrier_semaphore()
    peers = [along(by) for along in (along_x, along_y, along_z) for by in OFFSETS] + [partner]
    for peer in peers:
        pl.semaphore_signal(barrier, inc=1, device_id=peer, device_id_type=MESH)

    def bring(src, dst, sem):
        copy = pltpu.make_async_copy(src, dst, sem)
        copy.start()
        return copy

    def columns(h, part):
        return pl.ds(pl.multiple_of(h * HALF + part * PART, PART), PART)

    def rows(c):
        return pl.ds(STARTS[c], SIZES[c])

    panels = (v1_ref, v2_ref)
    both = range(2)
    own_v = [
        [bring(panels[p].at[:, columns(h, ring[h])], vbuf.at[h, p, x, y, k], loc_sem.at[2 * h + p]) for p in both]
        for h in both
    ]
    own_e = [
        [bring(e_ref.at[rows(c), columns(h, ring[h])], ebuf.at[h, ring[h], rows(c)], loc_sem.at[4 + 2 * c + h]) for h in both]
        for c in range(CHUNKS)
    ]
    at_t = 4 + 2 * CHUNKS
    own_t = [bring(t1_ref, t1, loc_sem.at[at_t]), bring(t2_ref, t2, loc_sem.at[at_t + 1])]

    pl.semaphore_wait(barrier, len(peers))

    m1 = [[None] * 3 for _ in both]
    for d, by in enumerate(OFFSETS):
        for h in both:
            m1[h][d] = [
                send(
                    panels[p].at[:, columns(h, shift(ring[h], by))],
                    vbuf.at[h, p, x, y, k],
                    m1_s.at[h, d, p], m1_r.at[h, d, p], ring_peer[h](by),
                )
                for p in both
            ]

    def piece(h, j, at):
        origin = ring[h] if j == 0 else shift(ring[h], 4 - OFFSETS[j - 1])
        return vbuf.at[h, :, origin, at, k] if h == 0 else vbuf.at[h, :, at, origin, k]

    m2 = [[[None] * 4 for _ in both] for _ in both]
    m3 = [[[None] * 4 for _ in both] for _ in both]
    dd = [[None] * 20 for _ in both]

    def mirror(h, src, at):
        dd[h][at] = send(src, src, dd_s.at[h, at], dd_r.at[h, at], partner)

    def cut(h, j, at, copies):
        origin = ring[h] if j == 0 else shift(ring[h], 4 - OFFSETS[j - 1])
        at_x, at_y = (origin, at) if h == 0 else (at, origin)
        for copy in copies:
            dd[h][copy].wait_recv()
        for p in both:
            to = pl.ds(pl.multiple_of(p * 256 + at_x * 64 + at_y * 16, 16), 16)
            vhigh[h, to, :], vlow[h, to, :] = split(vbuf[h, p, at_x, at_y].reshape(16, PART))

    def pass_on(h, j):
        src = piece(h, j, cross[h])
        for way, by in WAYS:
            m2[h][way][j] = send(src, src, m2_s.at[h, way, j], m2_r.at[h, way, j], cross_peer[h](by))
        mirror(h, src, j)

    def pass_further(h, j):
        for way, by in WAYS:
            m2[h][way][j].wait_recv()
            src = piece(h, j, shift(cross[h], 4 - by))
            part = src.at[way]
            m3[h][way][j] = send(part, part, m3_s.at[h, way, j], m3_r.at[h, way, j], cross_peer[h](by))
            mirror(h, src, 4 + 4 * way + j)

    def finish(h, j):
        for way, _ in WAYS:
            m3[h][way][j].wait_recv()
            mirror(h, piece(h, j, shift(cross[h], 2)).at[way], 12 + 4 * way + j)

    def arrived(h, d):
        for p in both:
            m1[h][d][p].wait_recv()
        pass_on(h, d + 1)

    moved = [[[None] * 3 for _ in both] for _ in range(CHUNKS)]

    def move(c):
        for d, by in enumerate(OFFSETS):
            for h in both:
                moved[c][h][d] = send(
                    e_ref.at[rows(c), columns(h, shift(ring[h], by))],
                    ebuf.at[h, ring[h], rows(c)],
                    e_s.at[c, h, d], e_r.at[c, h, d], ring_peer[h](by),
                )

    def cut_near(j):
        for h in both:
            cut(h, j, cross[h], [j])

    def cut_next(j):
        for h in both:
            for way, by in WAYS:
                cut(h, j, shift(cross[h], 4 - by), [4 + 4 * way + j])

    def cut_far(j):
        for h in both:
            cut(h, j, shift(cross[h], 2), [12 + j, 16 + j])

    for h in both:
        for copy in own_v[h]:
            copy.wait()
        pass_on(h, 0)
    for d in (0, 1):
        for h in both:
            arrived(h, d)
    for h in both:
        pass_further(h, 0)
    for h in both:
        arrived(h, 2)
    cut_near(0)
    cut_near(1)
    cut_near(2)
    for h in both:
        pass_further(h, 1)
    cut_near(3)
    for h in both:
        pass_further(h, 2)
    cut_next(0)
    cut_next(1)
    for h in both:
        pass_further(h, 3)
    for h in both:
        finish(h, 0)
    move(0)
    cut_next(2)
    for h in both:
        finish(h, 1)
    cut_next(3)
    for h in both:
        finish(h, 2)
    cut_far(0)
    for h in both:
        finish(h, 3)
    cut_far(1)
    cut_far(2)
    cut_far(3)

    g = [[None] * 3 for _ in both]
    for h in both:
        mine = vbuf[h, 0, :, y, k] if h == 0 else vbuf[h, 0, x, :, k]
        terms = products_of((vhigh[h, pl.ds(256, 256), :], vlow[h, pl.ds(256, 256), :]), split(mine.reshape(32, PART)))
        gsend[h] = terms.T.reshape(SIDE, 8, 256)
        for d, by in enumerate(OFFSETS):
            g[h][d] = send(
                gsend.at[h, shift(ring[h], by)], grecv.at[h, d], g_s.at[h, d], g_r.at[h, d], ring_peer[h](by)
            )

    def gram_rows():
        total = gsend[0, x] + gsend[1, y]
        for h in both:
            for d in range(3):
                g[h][d].wait_recv()
                total = total + grecv[h, d]
        gpart[z, x] = total
        mine = gpart.at[z, x]
        return [send(mine, mine, gz_s.at[d], gz_r.at[d], along_z(by)) for d, by in enumerate(OFFSETS)]

    def gram_spread(copies):
        for copy in copies:
            copy.wait_recv()
        gfull[x, y, k] = gpart[0, x] + gpart[1, x] + gpart[2, x] + gpart[3, x]
        mine = gfull.at[x, y, k]
        return [send(mine, mine, gz_s.at[3 + d], gz_r.at[3 + d], along_x(by)) for d, by in enumerate(OFFSETS)]

    def gram_sum(copies):
        for copy in copies:
            copy.wait_recv()
        mine = gfull.at[:, y, k]
        return [send(mine, mine, gp_s.at[d], gp_r.at[d], along_y(by)) for d, by in enumerate(OFFSETS)]

    def gram_partner(copies):
        for copy in copies:
            copy.wait_recv()
        mine = gfull.at[:, :, k]
        return [send(mine, mine, gp_s.at[3], gp_r.at[3], partner)]

    def gram_use(copies):
        for copy in copies:
            copy.wait_recv()
        t1_gram[...] = plain_full(t1[...], gfull[...].reshape(256, 256))

    w = [[[None] * 3 for _ in both] for _ in range(CHUNKS)]
    zs = [None] * CHUNKS
    xs = [[[None] * 3 for _ in both] for _ in range(CHUNKS)]
    back = []

    def products(c):
        terms = []
        for h in both:
            own_e[c][h].wait()
            for d in range(3):
                moved[c][h][d].wait_recv()
            vecs = split(ebuf[h, :, rows(c), :].reshape(SIDE * SIZES[c], PART))
            terms.append(products_of((vhigh[h], vlow[h]), vecs))
        psend[:, :, rows(c), :] = jnp.concatenate(terms, axis=1).T.reshape(2, SIDE, SIZES[c], 512)
        for h in both:
            for d, by in enumerate(OFFSETS):
                w[c][h][d] = send(
                    psend.at[h, shift(ring[h], by), rows(c)],
                    precv.at[h, d, rows(c)], w_s.at[c, h, d], w_r.at[c, h, d], ring_peer[h](by),
                )

    def plane_sum(c):
        total = psend[0, x, rows(c), :] + psend[1, y, rows(c), :]
        for h in both:
            for d in range(3):
                w[c][h][d].wait_recv()
                total = total + precv[h, d, rows(c), :]
        zsend[rows(c), :] = total
        zs[c] = [
            send(zsend.at[rows(c)], zrecv.at[d, rows(c)], z_s.at[c, d], z_r.at[c, d], along_z(by)) for d, by in enumerate(OFFSETS)
        ]

    def coefficients(c):
        total = zsend[rows(c), :]
        for copy in own_t if c == 0 else []:
            copy.wait()
        for d in range(3):
            zs[c][d].wait_recv()
            total = total + zrecv[d, rows(c), :]
        first, second = total[:, :256], total[:, 256:]
        coef_second = inner_full(second, t2[...])
        coef_first = inner_full(first, t1[...])
        for h in both:
            xbuf[h, ring[h], rows(c), pl.ds(0, 256)] = coef_first
            xbuf[h, ring[h], rows(c), pl.ds(256, 256)] = coef_second
        for h in both:
            mine = xbuf.at[h, ring[h], rows(c)]
            for d, by in enumerate(OFFSETS):
                xs[c][h][d] = send(mine, mine, x_s.at[c, h, d], x_r.at[c, h, d], ring_peer[h](by))

    def update(c):
        count = SIDE * SIZES[c]
        for h in both:
            for d in range(3):
                xs[c][h][d].wait_recv()
        first, second = (xbuf[:, :, rows(c), pl.ds(p * 256, 256)].reshape(2 * count, 256) for p in both)
        first = first - inner_full(second, t1_gram[...])
        high, low = split(jnp.concatenate([first, second], axis=1))
        for tile in range(TILES):
            cols = pl.ds(tile * TILE, TILE)
            for h in both:
                coefs = (high[h * count : (h + 1) * count], low[h * count : (h + 1) * count])
                change = combine(coefs, (vhigh[h, :, cols], vlow[h, :, cols]))
                obuf[h, :, rows(c), cols] = ebuf[h, :, rows(c), cols] - change.reshape(SIDE, SIZES[c], TILE)
                there = pl.ds(pl.multiple_of(h * HALF + ring[h] * PART + tile * TILE, TILE), TILE)
                for d, by in enumerate(OFFSETS):
                    back.append(
                        send(
                            obuf.at[h, shift(ring[h], by), rows(c), cols], out_ref.at[rows(c), there],
                            o_s.at[c, h, tile, d], o_r.at[c, h, tile, d], ring_peer[h](by),
                        )
                    )
                stays.append(bring(obuf.at[h, ring[h], rows(c), cols], out_ref.at[rows(c), there], own_sem.at[c, h, tile]))

    stays = []
    move(1)
    products(0)
    step = gram_rows()
    plane_sum(0)
    step = gram_spread(step)
    products(1)
    step = gram_sum(step)
    plane_sum(1)
    coefficients(0)
    step = gram_partner(step)
    gram_use(step)
    coefficients(1)
    update(0)
    update(1)
    for copy in back:
        copy.wait_recv()
    for copy in stays:
        copy.wait()
    for copy in sent:
        copy.wait_send()


def hand_over(src, dst, held, sems):
    spots = [(pl.ds(i * 8, 8), pl.ds(j * 8192, 8192)) for i in range(4) for j in range(2)]
    arriving = [pltpu.make_async_copy(src.at[spot], held.at[spot], sems.at[0, i]) for i, spot in enumerate(spots)]
    leaving = [pltpu.make_async_copy(held.at[spot], dst.at[spot], sems.at[1, i]) for i, spot in enumerate(spots)]
    for copy in arriving:
        copy.start()
    for came, copy in zip(arriving, leaving):
        came.wait()
        copy.start()
    for copy in leaving:
        copy.wait()


def shards(evecs, v_first, v_second, t_first, t_second):
    vmem = pltpu.VMEM
    dma = pltpu.SemaphoreType.DMA

    def both(*shape):
        return [dma(shape), dma(shape)]

    basis = pl.pallas_call(
        body,
        out_shape=jax.ShapeDtypeStruct(evecs.shape, evecs.dtype),
        in_specs=[pl.BlockSpec(memory_space=pl.ANY)] * 5,
        out_specs=pl.BlockSpec(memory_space=pl.ANY),
        scratch_shapes=[
            vmem((2, 2, 4, 4, 2, 8, PART), F32),
            vmem((2, 512, PART), BF16),
            vmem((2, 512, PART), BF16),
            vmem((2, SIDE, MINE, PART), F32),
            vmem((2, SIDE, MINE, PART), F32),
            vmem((256, 256), F32),
            vmem((256, 256), F32),
            vmem((256, 256), F32),
            vmem((2, SIDE, MINE, 512), F32),
            vmem((2, 3, MINE, 512), F32),
            vmem((MINE, 512), F32),
            vmem((3, MINE, 512), F32),
            vmem((2, SIDE, MINE, 512), F32),
            vmem((2, SIDE, 8, 256), F32),
            vmem((2, 3, 8, 256), F32),
            vmem((4, 4, 8, 256), F32),
            vmem((4, 4, 2, 8, 256), F32),
            dma((6 + 2 * CHUNKS,)),
            dma((CHUNKS, 2, TILES)),
            *both(2, 3, 2),
            *both(2, 2, 4),
            *both(2, 2, 4),
            *both(2, 20),
            *both(CHUNKS, 2, 3),
            *both(2, 3),
            *both(6),
            *both(4),
            *both(CHUNKS, 2, 3),
            *both(CHUNKS, 3),
            *both(CHUNKS, 2, 3),
            *both(CHUNKS, 2, TILES, 3),
        ],
        compiler_params=pltpu.CompilerParams(
            collective_id=0, has_side_effects=True, vmem_limit_bytes=56 << 20
        ),
        name="back_transform",
    )(evecs, v_first, v_second, t_first, t_second)
    return pl.pallas_call(
        hand_over,
        out_shape=jax.ShapeDtypeStruct(evecs.shape, evecs.dtype),
        in_specs=[pl.BlockSpec(memory_space=pl.ANY)],
        out_specs=pl.BlockSpec(memory_space=pl.ANY),
        scratch_shapes=[vmem(evecs.shape, F32), dma((2, 8))],
        compiler_params=pltpu.CompilerParams(vmem_limit_bytes=56 << 20),
        name="hand_over",
    )(basis)


def solution(mesh):
    placed = (P("col", "row"), P("col", "row"), P("col", "row"), P(), P())
    return jax.shard_map(
        shards, mesh=mesh, in_specs=placed, out_specs=P("col", "row"), check_vma=False
    )
```

```python
import jax
import jax.numpy as jnp
from jax import lax
from jax.experimental import pallas as pl
from jax.experimental.pallas import tpu as pltpu
from jax.sharding import PartitionSpec as P

MESH = pl.DeviceIdType.MESH
F32 = jnp.float32
BF16 = jnp.bfloat16
HIGHEST = lax.Precision.HIGHEST

SIDE = 4
HALF = 8192
PART = HALF // SIDE
MINE = 32
SIZES = (16, 16)
STARTS = tuple(sum(SIZES[:c]) for c in range(len(SIZES)))
CHUNKS = len(SIZES)
TILE = 1024
TILES = PART // TILE
OFFSETS = (1, 3, 2)
WAYS = ((0, 1), (1, 3))


def inner(left, right):
    return lax.dot_general(left, right, (((1,), (1,)), ((), ())), preferred_element_type=F32)


def plain(left, right):
    return jnp.dot(left, right, preferred_element_type=F32)


def plain_full(left, right):
    return jnp.dot(left, right, precision=HIGHEST, preferred_element_type=F32)


def split(value):
    high = value.astype(BF16)
    return high, (value - high.astype(F32)).astype(BF16)


def products_of(vectors, rows):
    count = rows[0].shape[0]
    high = inner(vectors[0], jnp.concatenate(rows, axis=0))
    return high[:, :count] + high[:, count:] + inner(vectors[1], rows[0])


def combine(coefs, vectors):
    count = coefs[0].shape[0]
    high = plain(jnp.concatenate(coefs, axis=0), vectors[0])
    return high[:count] + high[count:] + plain(coefs[0], vectors[1])


def body(
    e_ref, v1_ref, v2_ref, t1_ref, t2_ref, out_ref,
    vbuf, vhigh, vlow, ebuf, obuf, t1, t2, t1_gram,
    psend, precv, zsend, zrecv, xbuf,
    gsend, grecv, gpart, gfull,
    loc_sem, own_sem,
    m1_s, m1_r, m2_s, m2_r, m3_s, m3_r, dd_s, dd_r, e_s, e_r,
    g_s, g_r, gz_s, gz_r, gp_s, gp_r,
    w_s, w_r, z_s, z_r, x_s, x_r, o_s, o_r,
):
    col = lax.axis_index("col")
    z = lax.axis_index("row")
    x, y, k = col // 8, (col // 2) % 4, col % 2
    ring = (x, y)
    cross = (y, x)

    def shift(at, by):
        return lax.rem(at + by, SIDE)

    def device(dx=0, dy=0, dz=0, dk=0):
        return (shift(z, dz), shift(x, dx) * 8 + shift(y, dy) * 2 + lax.rem(k + dk, 2))

    def along_x(by):
        return device(dx=by)

    def along_y(by):
        return device(dy=by)

    def along_z(by):
        return device(dz=by)

    partner = device(dk=1)
    ring_peer = (along_x, along_y)
    cross_peer = (along_y, along_x)

    sent = []

    def send(src, dst, s, r, to):
        copy = pltpu.make_async_remote_copy(
            src_ref=src, dst_ref=dst, send_sem=s, recv_sem=r, device_id=to, device_id_type=MESH
        )
        copy.start()
        sent.append(copy)
        return copy

    barrier = pltpu.get_barrier_semaphore()
    peers = [along(by) for along in (along_x, along_y, along_z) for by in OFFSETS] + [partner]
    for peer in peers:
        pl.semaphore_signal(barrier, inc=1, device_id=peer, device_id_type=MESH)

    def bring(src, dst, sem):
        copy = pltpu.make_async_copy(src, dst, sem)
        copy.start()
        return copy

    def columns(h, part):
        return pl.ds(pl.multiple_of(h * HALF + part * PART, PART), PART)

    def rows(c):
        return pl.ds(STARTS[c], SIZES[c])

    panels = (v1_ref, v2_ref)
    both = range(2)
    own_v = [
        [bring(panels[p].at[:, columns(h, ring[h])], vbuf.at[h, p, x, y, k], loc_sem.at[2 * h + p]) for p in both]
        for h in both
    ]
    own_e = [
        [bring(e_ref.at[rows(c), columns(h, ring[h])], ebuf.at[h, ring[h], rows(c)], loc_sem.at[4 + 2 * c + h]) for h in both]
        for c in range(CHUNKS)
    ]
    at_t = 4 + 2 * CHUNKS
    own_t = [bring(t1_ref, t1, loc_sem.at[at_t]), bring(t2_ref, t2, loc_sem.at[at_t + 1])]

    pl.semaphore_wait(barrier, len(peers))

    m1 = [[None] * 3 for _ in both]
    for d, by in enumerate(OFFSETS):
        for h in both:
            m1[h][d] = [
                send(
                    panels[p].at[:, columns(h, shift(ring[h], by))],
                    vbuf.at[h, p, x, y, k],
                    m1_s.at[h, d, p], m1_r.at[h, d, p], ring_peer[h](by),
                )
                for p in both
            ]

    def piece(h, j, at):
        origin = ring[h] if j == 0 else shift(ring[h], 4 - OFFSETS[j - 1])
        return vbuf.at[h, :, origin, at, k] if h == 0 else vbuf.at[h, :, at, origin, k]

    m2 = [[[None] * 4 for _ in both] for _ in both]
    m3 = [[[None] * 4 for _ in both] for _ in both]
    dd = [[None] * 20 for _ in both]

    def mirror(h, src, at):
        dd[h][at] = send(src, src, dd_s.at[h, at], dd_r.at[h, at], partner)

    def cut(h, j, at, copies):
        origin = ring[h] if j == 0 else shift(ring[h], 4 - OFFSETS[j - 1])
        at_x, at_y = (origin, at) if h == 0 else (at, origin)
        for copy in copies:
            dd[h][copy].wait_recv()
        for p in both:
            to = pl.ds(pl.multiple_of(p * 256 + at_x * 64 + at_y * 16, 16), 16)
            vhigh[h, to, :], vlow[h, to, :] = split(vbuf[h, p, at_x, at_y].reshape(16, PART))

    def pass_on(h, j):
        src = piece(h, j, cross[h])
        for way, by in WAYS:
            m2[h][way][j] = send(src, src, m2_s.at[h, way, j], m2_r.at[h, way, j], cross_peer[h](by))
        mirror(h, src, j)

    def pass_further(h, j):
        for way, by in WAYS:
            m2[h][way][j].wait_recv()
            src = piece(h, j, shift(cross[h], 4 - by))
            part = src.at[way]
            m3[h][way][j] = send(part, part, m3_s.at[h, way, j], m3_r.at[h, way, j], cross_peer[h](by))
            mirror(h, src, 4 + 4 * way + j)

    def finish(h, j):
        for way, _ in WAYS:
            m3[h][way][j].wait_recv()
            mirror(h, piece(h, j, shift(cross[h], 2)).at[way], 12 + 4 * way + j)

    def arrived(h, d):
        for p in both:
            m1[h][d][p].wait_recv()
        pass_on(h, d + 1)

    moved = [[[None] * 3 for _ in both] for _ in range(CHUNKS)]

    def move(c):
        for d, by in enumerate(OFFSETS):
            for h in both:
                moved[c][h][d] = send(
                    e_ref.at[rows(c), columns(h, shift(ring[h], by))],
                    ebuf.at[h, ring[h], rows(c)],
                    e_s.at[c, h, d], e_r.at[c, h, d], ring_peer[h](by),
                )

    def cut_near(j):
        for h in both:
            cut(h, j, cross[h], [j])

    def cut_next(j):
        for h in both:
            for way, by in WAYS:
                cut(h, j, shift(cross[h], 4 - by), [4 + 4 * way + j])

    def cut_far(j):
        for h in both:
            cut(h, j, shift(cross[h], 2), [12 + j, 16 + j])

    for h in both:
        for copy in own_v[h]:
            copy.wait()
        pass_on(h, 0)
    for d in (0, 1):
        for h in both:
            arrived(h, d)
    for h in both:
        pass_further(h, 0)
    for h in both:
        arrived(h, 2)
    cut_near(0)
    cut_near(1)
    cut_near(2)
    for h in both:
        pass_further(h, 1)
    cut_near(3)
    for h in both:
        pass_further(h, 2)
    cut_next(0)
    cut_next(1)
    for h in both:
        pass_further(h, 3)
    for h in both:
        finish(h, 0)
    move(0)
    cut_next(2)
    for h in both:
        finish(h, 1)
    cut_next(3)
    for h in both:
        finish(h, 2)
    cut_far(0)
    for h in both:
        finish(h, 3)
    cut_far(1)
    cut_far(2)
    cut_far(3)

    g = [[None] * 3 for _ in both]
    for h in both:
        mine = vbuf[h, 0, :, y, k] if h == 0 else vbuf[h, 0, x, :, k]
        terms = products_of((vhigh[h, pl.ds(256, 256), :], vlow[h, pl.ds(256, 256), :]), split(mine.reshape(32, PART)))
        gsend[h] = terms.T.reshape(SIDE, 8, 256)
        for d, by in enumerate(OFFSETS):
            g[h][d] = send(
                gsend.at[h, shift(ring[h], by)], grecv.at[h, d], g_s.at[h, d], g_r.at[h, d], ring_peer[h](by)
            )

    def gram_rows():
        total = gsend[0, x] + gsend[1, y]
        for h in both:
            for d in range(3):
                g[h][d].wait_recv()
                total = total + grecv[h, d]
        gpart[z, x] = total
        mine = gpart.at[z, x]
        return [send(mine, mine, gz_s.at[d], gz_r.at[d], along_z(by)) for d, by in enumerate(OFFSETS)]

    def gram_spread(copies):
        for copy in copies:
            copy.wait_recv()
        gfull[x, y, k] = gpart[0, x] + gpart[1, x] + gpart[2, x] + gpart[3, x]
        mine = gfull.at[x, y, k]
        return [send(mine, mine, gz_s.at[3 + d], gz_r.at[3 + d], along_x(by)) for d, by in enumerate(OFFSETS)]

    def gram_sum(copies):
        for copy in copies:
            copy.wait_recv()
        mine = gfull.at[:, y, k]
        return [send(mine, mine, gp_s.at[d], gp_r.at[d], along_y(by)) for d, by in enumerate(OFFSETS)]

    def gram_partner(copies):
        for copy in copies:
            copy.wait_recv()
        mine = gfull.at[:, :, k]
        return [send(mine, mine, gp_s.at[3], gp_r.at[3], partner)]

    def gram_use(copies):
        for copy in copies:
            copy.wait_recv()
        t1_gram[...] = plain_full(t1[...].T, gfull[...].reshape(256, 256)).T

    w = [[[None] * 3 for _ in both] for _ in range(CHUNKS)]
    zs = [None] * CHUNKS
    xs = [[[None] * 3 for _ in both] for _ in range(CHUNKS)]
    back = []

    def products(c):
        terms = []
        for h in both:
            own_e[c][h].wait()
            for d in range(3):
                moved[c][h][d].wait_recv()
            vecs = split(ebuf[h, :, rows(c), :].reshape(SIDE * SIZES[c], PART))
            terms.append(products_of((vhigh[h], vlow[h]), vecs))
        psend[:, :, rows(c), :] = jnp.concatenate(terms, axis=1).T.reshape(2, SIDE, SIZES[c], 512)
        for h in both:
            for d, by in enumerate(OFFSETS):
                w[c][h][d] = send(
                    psend.at[h, shift(ring[h], by), rows(c)],
                    precv.at[h, d, rows(c)], w_s.at[c, h, d], w_r.at[c, h, d], ring_peer[h](by),
                )

    def plane_sum(c):
        total = psend[0, x, rows(c), :] + psend[1, y, rows(c), :]
        for h in both:
            for d in range(3):
                w[c][h][d].wait_recv()
                total = total + precv[h, d, rows(c), :]
        zsend[rows(c), :] = total
        zs[c] = [
            send(zsend.at[rows(c)], zrecv.at[d, rows(c)], z_s.at[c, d], z_r.at[c, d], along_z(by)) for d, by in enumerate(OFFSETS)
        ]

    def coefficients(c):
        total = zsend[rows(c), :]
        for d in range(3):
            zs[c][d].wait_recv()
            total = total + zrecv[d, rows(c), :]
        first, second = total[:, :256], total[:, 256:]
        coef_second = plain_full(second, t2[...])
        coef_first = plain_full(first, t1[...])
        for h in both:
            xbuf[h, ring[h], rows(c), pl.ds(0, 256)] = coef_first
            xbuf[h, ring[h], rows(c), pl.ds(256, 256)] = coef_second
        for h in both:
            mine = xbuf.at[h, ring[h], rows(c)]
            for d, by in enumerate(OFFSETS):
                xs[c][h][d] = send(mine, mine, x_s.at[c, h, d], x_r.at[c, h, d], ring_peer[h](by))

    def update(c):
        count = SIDE * SIZES[c]
        for h in both:
            for d in range(3):
                xs[c][h][d].wait_recv()
        first, second = (xbuf[:, :, rows(c), pl.ds(p * 256, 256)].reshape(2 * count, 256) for p in both)
        first = first - plain_full(second, t1_gram[...])
        high, low = split(jnp.concatenate([first, second], axis=1))
        for tile in range(TILES):
            cols = pl.ds(tile * TILE, TILE)
            for h in both:
                coefs = (high[h * count : (h + 1) * count], low[h * count : (h + 1) * count])
                change = combine(coefs, (vhigh[h, :, cols], vlow[h, :, cols]))
                obuf[h, :, rows(c), cols] = ebuf[h, :, rows(c), cols] - change.reshape(SIDE, SIZES[c], TILE)
                there = pl.ds(pl.multiple_of(h * HALF + ring[h] * PART + tile * TILE, TILE), TILE)
                for d, by in enumerate(OFFSETS):
                    back.append(
                        send(
                            obuf.at[h, shift(ring[h], by), rows(c), cols], out_ref.at[rows(c), there],
                            o_s.at[c, h, tile, d], o_r.at[c, h, tile, d], ring_peer[h](by),
                        )
                    )
                stays.append(bring(obuf.at[h, ring[h], rows(c), cols], out_ref.at[rows(c), there], own_sem.at[c, h, tile]))

    stays = []
    move(1)
    for copy, factor in zip(own_t, (t1, t2)):
        copy.wait()
        factor[...] = factor[...].T
    products(0)
    step = gram_rows()
    plane_sum(0)
    step = gram_spread(step)
    products(1)
    step = gram_sum(step)
    plane_sum(1)
    coefficients(0)
    step = gram_partner(step)
    gram_use(step)
    coefficients(1)
    update(0)
    update(1)
    for copy in back:
        copy.wait_recv()
    for copy in stays:
        copy.wait()
    for copy in sent:
        copy.wait_send()


def hand_over(src, dst, held, sems):
    spots = [(pl.ds(i * 8, 8), pl.ds(j * 8192, 8192)) for i in range(4) for j in range(2)]
    arriving = [pltpu.make_async_copy(src.at[spot], held.at[spot], sems.at[0, i]) for i, spot in enumerate(spots)]
    leaving = [pltpu.make_async_copy(held.at[spot], dst.at[spot], sems.at[1, i]) for i, spot in enumerate(spots)]
    for copy in arriving:
        copy.start()
    for came, copy in zip(arriving, leaving):
        came.wait()
        copy.start()
    for copy in leaving:
        copy.wait()


def shards(evecs, v_first, v_second, t_first, t_second):
    vmem = pltpu.VMEM
    dma = pltpu.SemaphoreType.DMA

    def both(*shape):
        return [dma(shape), dma(shape)]

    basis = pl.pallas_call(
        body,
        out_shape=jax.ShapeDtypeStruct(evecs.shape, evecs.dtype),
        in_specs=[pl.BlockSpec(memory_space=pl.ANY)] * 5,
        out_specs=pl.BlockSpec(memory_space=pl.ANY),
        scratch_shapes=[
            vmem((2, 2, 4, 4, 2, 8, PART), F32),
            vmem((2, 512, PART), BF16),
            vmem((2, 512, PART), BF16),
            vmem((2, SIDE, MINE, PART), F32),
            vmem((2, SIDE, MINE, PART), F32),
            vmem((256, 256), F32),
            vmem((256, 256), F32),
            vmem((256, 256), F32),
            vmem((2, SIDE, MINE, 512), F32),
            vmem((2, 3, MINE, 512), F32),
            vmem((MINE, 512), F32),
            vmem((3, MINE, 512), F32),
            vmem((2, SIDE, MINE, 512), F32),
            vmem((2, SIDE, 8, 256), F32),
            vmem((2, 3, 8, 256), F32),
            vmem((4, 4, 8, 256), F32),
            vmem((4, 4, 2, 8, 256), F32),
            dma((6 + 2 * CHUNKS,)),
            dma((CHUNKS, 2, TILES)),
            *both(2, 3, 2),
            *both(2, 2, 4),
            *both(2, 2, 4),
            *both(2, 20),
            *both(CHUNKS, 2, 3),
            *both(2, 3),
            *both(6),
            *both(4),
            *both(CHUNKS, 2, 3),
            *both(CHUNKS, 3),
            *both(CHUNKS, 2, 3),
            *both(CHUNKS, 2, TILES, 3),
        ],
        compiler_params=pltpu.CompilerParams(
            collective_id=0, has_side_effects=True, vmem_limit_bytes=56 << 20
        ),
        name="back_transform",
    )(evecs, v_first, v_second, t_first, t_second)
    return pl.pallas_call(
        hand_over,
        out_shape=jax.ShapeDtypeStruct(evecs.shape, evecs.dtype),
        in_specs=[pl.BlockSpec(memory_space=pl.ANY)],
        out_specs=pl.BlockSpec(memory_space=pl.ANY),
        scratch_shapes=[vmem(evecs.shape, F32), dma((2, 8))],
        compiler_params=pltpu.CompilerParams(vmem_limit_bytes=56 << 20),
        name="hand_over",
    )(basis)


def solution(mesh):
    placed = (P("col", "row"), P("col", "row"), P("col", "row"), P(), P())
    return jax.shard_map(
        shards, mesh=mesh, in_specs=placed, out_specs=P("col", "row"), check_vma=False
    )
```
